512 devices in a mesh: row: 16 (over x_hi, y, core), col: 32 (over z, x_lo).
Axes of the slice: x: 4 (x_hi: 2, x_lo: 2; x = x_hi * 2 + x_lo), y: 4, z: 16, core: 2. Of those that a mesh axis runs over, the one named last changes fastest.
Arguments:
- left_panel: bfloat16 [256, 512, 32], P('col', 'row'), may hold values from -6 to 6
- right_panel: bfloat16 [256, 512, 32], P('row', 'col'), may hold values from -6 to 6
- pair_grad: bfloat16 [512, 512, 128], P('row', 'col'), may hold values from -24 to 24
- out_weight: bfloat16 [1024, 128], replicated, may hold values from -0.1875 to 0.1875
Outputs:
- left_grad: float32 [256, 512, 32], P('col', 'row')
- right_grad: float32 [256, 512, 32], P('row', 'col')
- weight_grad: float32 [1024, 128], replicated
The draws below stay inside these ranges and needn't reach their ends.
All inputs are finite; a program needn't handle non-finite values.
Results may differ from the reference program's by a relative error of at most 0.0033.
Values may be sent and summed in bfloat16 or wider, within the bound.
A program may use at most 64 MiB of HBM per device.

```python
import jax
import jax.numpy as jnp
from jax import lax

N = 512
S = 256
C = 32
P_SIZE = 128


def block_scale(rng, dims, split, smallest, high):
    def one(axis_at, shards_of):
        steps = jax.random.uniform(jax.random.fold_in(jax.random.fold_in(rng, 6), axis_at), (shards_of,), jnp.float32, smallest / len(split), high / len(split))
        return jnp.repeat(jnp.exp(steps), dims[axis_at] // shards_of).reshape((-1,) + (1,) * (len(dims) - axis_at - 1))

    gain = one(*split[0])
    for cut in split[1:]:
        gain = gain * one(*cut)
    return gain


def scatter_about(own_key, extent, spread, limit, pieces=(), kind=jnp.bfloat16):
    array = spread * jax.random.normal(own_key, extent, jnp.float32)
    if pieces:
        array = array * block_scale(own_key, extent, pieces, -0.22, 0.18)
    return jnp.clip(array, -limit, limit).astype(kind)


def setup_inputs(seed: int = 0) -> dict:
    seeds = jax.random.split(jax.random.key(seed), 5)
    return {
        "left_panel": scatter_about(seeds[0], (S, N, C), 1.0, 6.0, ((0, 32), (1, 16))),
        "right_panel": scatter_about(seeds[1], (S, N, C), 1.0, 6.0, ((0, 16), (1, 32))),
        "pair_grad": scatter_about(seeds[2], (N, N, P_SIZE), 4.0, 24.0, ((0, 16), (1, 32))),
        "out_weight": scatter_about(seeds[3], (C * C, P_SIZE), (C * C) ** -0.5, 0.1875),
    }


def reference(left_panel, right_panel, pair_grad, out_weight):
    block_rows = N // 16
    right_flat = right_panel.reshape(S, N * C)
    weight_t = out_weight.T

    def advance(carried, block_index):
        right_acc, weight_acc = carried
        first_row = (block_index * block_rows).astype(jnp.int32)
        grad_rows = lax.dynamic_slice_in_dim(pair_grad, first_row, block_rows, 0).reshape(block_rows * N, P_SIZE)
        left_rows = lax.dynamic_slice_in_dim(left_panel, first_row, block_rows, 1).reshape(S, block_rows * C)
        expanded = (jnp.dot(grad_rows, weight_t, preferred_element_type=jnp.float32) / S).astype(jnp.bfloat16)
        expanded = expanded.reshape(block_rows, N, C, C).transpose(0, 2, 1, 3).reshape(block_rows * C, N * C)
        left_term = lax.dot_general(right_flat, expanded, (((1,), (1,)), ((), ())), preferred_element_type=jnp.float32)
        right_acc = right_acc + jnp.dot(left_rows, expanded, preferred_element_type=jnp.float32)
        outer_prod = lax.dot_general(left_rows, right_flat, (((0,), (0,)), ((), ())), preferred_element_type=jnp.float32)
        outer_prod = (outer_prod / S).astype(jnp.bfloat16)
        outer_prod = outer_prod.reshape(block_rows, C, N, C).transpose(0, 2, 1, 3).reshape(block_rows * N, C * C)
        weight_acc = weight_acc + lax.dot_general(outer_prod, grad_rows, (((0,), (0,)), ((), ())), preferred_element_type=jnp.float32)
        return (right_acc, weight_acc), left_term

    start_state = (jnp.zeros((S, N * C), jnp.float32), jnp.zeros((C * C, P_SIZE), jnp.float32))
    (right_acc, weight_acc), left_terms = lax.scan(advance, start_state, jnp.arange(16, dtype=jnp.int32))
    left_grad = left_terms.reshape(16, S, block_rows, C).transpose(1, 0, 2, 3).reshape(S, N, C)
    right_grad = right_acc.reshape(S, N, C)
    return left_grad, right_grad, weight_acc / N
```

```python
import functools

import jax
import jax.numpy as jnp
from jax import lax
from jax.experimental import pallas as pl
from jax.experimental.pallas import tpu as pltpu
from jax.sharding import PartitionSpec as P

MESH = pl.DeviceIdType.MESH
F32, BF = jnp.float32, jnp.bfloat16
ROWS, ZS, XL = 16, 16, 2
COLS = ZS * XL
PLANE = ROWS * XL


def swap4(x):
    lane = lax.broadcasted_iota(jnp.int32, x[0].shape, 1)
    low = lane < 64
    even = (lane // 32) % 2 == 0
    r = [pltpu.roll(v, 64, 1) for v in x]
    a = [
        jnp.where(low, x[0], r[2]),
        jnp.where(low, x[1], r[3]),
        jnp.where(low, r[0], x[2]),
        jnp.where(low, r[1], x[3]),
    ]
    y = []
    for p in (0, 2):
        y.append(jnp.where(even, a[p], pltpu.roll(a[p + 1], 32, 1)))
        y.append(jnp.where(even, pltpu.roll(a[p], 96, 1), a[p + 1]))
    return y


def expand(g, w, tile, ef, eb):
    def part(a, _):
        rows = pl.ds(pl.multiple_of(a * 128, 128), 128)
        tile[...] = lax.dot_general(
            g[...], w[rows, :], (((1,), (1,)), ((), ())), preferred_element_type=F32
        ) * (1.0 / 256)
        for jg in range(4):
            for i0 in range(4):
                x = [tile[pl.ds(i0 * 128 + 4 * jg + b, 8, stride=16), :] for b in range(4)]
                y = swap4(x)
                for q in range(4):
                    ef[jg, pl.ds(i0 * 256 + 4 * a + q, 8, stride=32), :] = y[q]
        return 0

    lax.fori_loop(0, 8, part, 0)

    def cast(t, _):
        rows = pl.ds(pl.multiple_of(t * 128, 128), 128)
        for jg in range(4):
            eb[rows, jg * 128 : (jg + 1) * 128] = ef[jg, rows, :].astype(BF)
        return 0

    lax.fori_loop(0, 8, cast, 0)


def left_term(rg, eb, out):
    def part(t, _):
        rows = pl.ds(pl.multiple_of(t * 256, 256), 256)
        v = lax.dot_general(rg[...], eb[rows, :], (((1,), (1,)), ((), ())), preferred_element_type=F32)
        out[:, :, rows] = v.reshape(32, 8, 256).astype(BF)
        return 0

    lax.fori_loop(0, 4, part, 0)


def right_term(lg, eb, out):
    def part(t, _):
        cols = pl.ds(pl.multiple_of(t * 256, 256), 256)
        v = jnp.dot(lg[...], eb[:, cols], preferred_element_type=F32)
        out[:, :, cols] = v.reshape(16, 16, 256).astype(BF)
        return 0

    lax.fori_loop(0, 2, part, 0)


def outer_part(lg, rg, of):
    def part(t, _):
        cols = pl.ds(pl.multiple_of(t * 256, 256), 256)
        for h in range(2):
            v = lax.dot_general(
                lg[:, cols],
                rg[:, h * 256 : (h + 1) * 256],
                (((0,), (0,)), ((), ())),
                preferred_element_type=F32,
            ) * (1.0 / 256)
            of[2 * h, cols, :] = v[:, :128]
            of[2 * h + 1, cols, :] = v[:, 128:]
        return 0

    lax.fori_loop(0, 4, part, 0)


def weight_part(g, of, tile, out):
    def part(a, _):
        for jg in range(4):
            for i0 in range(4):
                x = [of[jg, pl.ds(i0 * 256 + 4 * a + q, 8, stride=32), :] for q in range(4)]
                y = swap4(x)
                for b in range(4):
                    tile[pl.ds(i0 * 128 + 4 * jg + b, 8, stride=16), :] = y[b]
        v = lax.dot_general(
            tile[...].astype(BF), g[...], (((0,), (0,)), ((), ())), preferred_element_type=F32
        )
        out[pl.ds(a * 4, 4)] = v.reshape(4, 32, 128).astype(BF)
        return 0

    lax.fori_loop(0, 8, part, 0)


def kernel(
    l_hbm, r_hbm, g_hbm, w_hbm, lo, ro, wo,
    lv, rv, gv, wv, lf, rf, lflat, rflat, g2,
    lb, rb, lg, rg, tile, ef, eb, of,
    sl, rl, sr, rr, sw, rw, zb, ab,
    in_sem, ag_l, ag_r, rs_l, rs_r, rs_w, z_w, ag_w,
):
    row, col = lax.axis_index("row"), lax.axis_index("col")
    z, xl = col // XL, col % XL
    plane = xl * ROWS + row

    def col_at(k):
        c = ((z + k // XL) % ZS) * XL + (xl + k % XL) % XL
        return {"row": row, "col": c}, c

    def row_at(k):
        r = (row + k) % ROWS
        return {"row": r, "col": col}, r

    def plane_at(k):
        r, x = (row + k % ROWS) % ROWS, (xl + k // ROWS) % XL
        return {"row": r, "col": z * XL + x}, x * ROWS + r

    def z_at(k):
        zz = (z + k) % ZS
        return {"row": row, "col": zz * XL + xl}, zz

    inputs = [
        pltpu.make_async_copy(src, dst, in_sem.at[n])
        for n, (src, dst) in enumerate(((l_hbm, lv), (r_hbm, rv), (g_hbm, gv), (w_hbm, wv)))
    ]
    for c in inputs:
        c.start()

    barrier = pltpu.get_barrier_semaphore()

    def greet(at, first, last):
        def one(k, _):
            pl.semaphore_signal(barrier, inc=1, device_id=at(k)[0], device_id_type=MESH)
            return 0

        lax.fori_loop(first, last, one, 0)

    greet(col_at, 1, COLS)
    greet(row_at, 1, ROWS)
    greet(plane_at, ROWS + 1, PLANE)

    inputs[0].wait()
    inputs[1].wait()
    lf[...] = lv[...].reshape(256, 32).astype(F32)
    rf[...] = rv[...].reshape(256, 32).astype(F32)
    for i in range(32):
        lflat[:, 32 * i : 32 * i + 32] = lf[pl.ds(i, 8, stride=32), :]
    for j in range(16):
        rflat[:, 32 * j : 32 * j + 32] = rf[pl.ds(j, 16, stride=16), :]
    lb[col] = lflat[...].astype(BF)
    rb[row] = rflat[...].astype(BF)

    inputs[2].wait()
    inputs[3].wait()
    g2[...] = gv[...].reshape(512, 128)
    expand(g2, wv, tile, ef, eb)

    pl.semaphore_wait(barrier, COLS - 1 + ROWS - 1 + PLANE - ROWS - 1)

    def copies(at, n, src_slot, dst_slot, sems):
        def make(k):
            where, slot = at(k)
            return pltpu.make_async_remote_copy(
                src_ref=src_slot(slot),
                dst_ref=dst_slot,
                send_sem=sems.at[0, k],
                recv_sem=sems.at[1, k],
                device_id=where,
                device_id_type=MESH,
            )

        def each(act):
            def one(k, _):
                act(make(k))
                return 0

            lax.fori_loop(1, n, one, 0)

        return (
            lambda: each(lambda c: c.start()),
            lambda: each(lambda c: c.wait_recv()),
            lambda: each(lambda c: c.wait_send()),
        )

    ag_r_start, ag_r_recv, ag_r_sent = copies(row_at, ROWS, lambda s: rb.at[row], rb.at[row], ag_r)
    ag_l_start, ag_l_recv, ag_l_sent = copies(col_at, COLS, lambda s: lb.at[col], lb.at[col], ag_l)
    rs_l_start, rs_l_recv, rs_l_sent = copies(col_at, COLS, lambda s: sl.at[s], rl.at[col], rs_l)
    rs_r_start, rs_r_recv, rs_r_sent = copies(row_at, ROWS, lambda s: sr.at[s], rr.at[row], rs_r)
    rs_w_start, rs_w_recv, rs_w_sent = copies(plane_at, PLANE, lambda s: sw.at[s], rw.at[plane], rs_w)
    z_w_start, z_w_recv, z_w_sent = copies(z_at, ZS, lambda s: zb.at[z], zb.at[z], z_w)
    ag_w_start, ag_w_recv, ag_w_sent = copies(plane_at, PLANE, lambda s: ab.at[plane], ab.at[plane], ag_w)

    ag_r_start()
    ag_l_start()
    ag_r_recv()
    rg[...] = rb[...].reshape(256, 512)
    left_term(rg, eb, sl)
    rs_l_start()
    rl[col] = sl[col]
    ag_l_recv()
    lg[...] = lb[...].astype(F32).reshape(256, 1024).astype(BF)
    outer_part(lg, rg, of)
    weight_part(g2, of, tile, sw)
    rs_w_start()
    rw[plane] = sw[plane]
    right_term(lg, eb, sr)
    rs_r_start()
    rr[row] = sr[row]
    rs_w_recv()
    zb[z] = jnp.sum(rw[...].astype(F32), axis=0).astype(BF)
    z_w_start()
    rs_r_recv()
    rflat[...] = jnp.sum(rr[...].astype(F32), axis=0)
    for j in range(16):
        ro[:, j, :] = rflat[:, 32 * j : 32 * j + 32]
    z_w_recv()
    ab[plane] = jnp.sum(zb[...].astype(F32), axis=0).astype(BF)
    ag_w_start()
    rs_l_recv()
    lflat[...] = jnp.sum(rl[...].astype(F32), axis=0)
    for i in range(32):
        lo[:, i, :] = lflat[:, 32 * i : 32 * i + 32]
    ag_w_recv()
    wo[...] = ab[...].astype(F32).reshape(1024, 128) * (1.0 / 512)
    for done in (ag_r_sent, ag_l_sent, rs_l_sent, rs_r_sent, rs_w_sent, z_w_sent, ag_w_sent):
        done()


def per_device(left_panel, right_panel, pair_grad, out_weight):
    V = pltpu.VMEM
    dma = pltpu.SemaphoreType.DMA
    return pl.pallas_call(
        kernel,
        out_shape=[
            jax.ShapeDtypeStruct((8, 32, 32), F32),
            jax.ShapeDtypeStruct((16, 16, 32), F32),
            jax.ShapeDtypeStruct((1024, 128), F32),
        ],
        in_specs=[pl.BlockSpec(memory_space=pltpu.HBM)] * 4,
        out_specs=[pl.BlockSpec(memory_space=V)] * 3,
        scratch_shapes=[
            V((8, 32, 32), BF), V((16, 16, 32), BF), V((32, 16, 128), BF), V((1024, 128), BF),
            V((256, 32), F32), V((256, 32), F32), V((8, 1024), F32), V((16, 512), F32), V((512, 128), BF),
            V((32, 8, 1024), BF), V((16, 16, 512), BF), V((256, 1024), BF), V((256, 512), BF),
            V((512, 128), F32), V((4, 1024, 128), F32), V((1024, 512), BF), V((4, 1024, 128), F32),
            V((32, 8, 1024), BF), V((32, 8, 1024), BF), V((16, 16, 512), BF), V((16, 16, 512), BF),
            V((32, 32, 128), BF), V((32, 32, 128), BF), V((16, 32, 128), BF), V((32, 32, 128), BF),
            dma((4,)), dma((2, 32)), dma((2, 16)), dma((2, 32)), dma((2, 16)), dma((2, 32)), dma((2, 16)), dma((2, 32)),
        ],
        compiler_params=pltpu.CompilerParams(
            collective_id=0, has_side_effects=True, vmem_limit_bytes=48 << 20
        ),
        cost_estimate=pl.CostEstimate(flops=1 << 30, bytes_accessed=1 << 20, transcendentals=0),
        name="pair_backward",
    )(left_panel, right_panel, pair_grad, out_weight)


def solution(mesh):
    in_specs = (P("col", "row", None), P("row", "col", None), P("row", "col", None), P())
    out_specs = (P("col", "row", None), P("row", "col", None), P())
    return jax.shard_map(
        per_device, mesh=mesh, in_specs=in_specs, out_specs=out_specs, check_vma=False
    )
```

```python
import jax
import jax.numpy as jnp
from jax import lax
from jax.experimental import pallas as pl
from jax.experimental.pallas import tpu as pltpu
from jax.sharding import PartitionSpec as P

MESH = pl.DeviceIdType.MESH
F32, BF = jnp.float32, jnp.bfloat16
ROWS, ZS, XL = 16, 16, 2
COLS = ZS * XL
PLANE = ROWS * XL
NEAR = ((2, 0), (2, 1), (1, 1), (-1, 1), (1, 0), (-1, 0), (0, 1))
GREETED = len(NEAR) + 2 + (ROWS - 1) + (ROWS - 1)


def swap4(x):
    lane = lax.broadcasted_iota(jnp.int32, x[0].shape, 1)
    low = lane < 64
    even = (lane // 32) % 2 == 0
    r = [pltpu.roll(v, 64, 1) for v in x]
    a = [
        jnp.where(low, x[0], r[2]),
        jnp.where(low, x[1], r[3]),
        jnp.where(low, r[0], x[2]),
        jnp.where(low, r[1], x[3]),
    ]
    y = []
    for p in (0, 2):
        y.append(jnp.where(even, a[p], pltpu.roll(a[p + 1], 32, 1)))
        y.append(jnp.where(even, pltpu.roll(a[p], 96, 1), a[p + 1]))
    return y


def expand(gji, w, eb):
    wd = 256

    def part(a, _):
        w_rows = w[pl.ds(pl.multiple_of(a * wd, wd), wd), :]
        m = lax.dot_general(gji[...], w_rows, (((1,), (1,)), ((), ())), preferred_element_type=F32)
        m = (m * (1.0 / 256)).astype(BF)
        for h in range(wd // 128):
            for jg in range(4):
                for i0 in range(2):
                    x = []
                    for b in range(4):
                        r0 = (4 * jg + b) * 32 + 16 * i0
                        x.append(m[r0 : r0 + 16, 128 * h : 128 * h + 128])
                    y = swap4(x)
                    for q in range(4):
                        r0 = pl.multiple_of(a * wd + h * 128 + q * 32 + 16 * i0, 16)
                        eb[pl.ds(r0, 16), 128 * jg : 128 * jg + 128] = y[q]
        return 0

    lax.fori_loop(0, 1024 // wd, part, 0, unroll=4)


def left_term(rg, eb, out):
    wd = 256

    def part(t, _):
        rows = pl.ds(pl.multiple_of(t * wd, wd), wd)
        v = lax.dot_general(rg[...], eb[rows, :], (((1,), (1,)), ((), ())), preferred_element_type=F32)
        for m in range(4):
            out[:, :, m, :, rows] = v[64 * m : 64 * m + 64].reshape(4, 2, 8, wd).astype(BF)
        return 0

    lax.fori_loop(0, 1024 // wd, part, 0, unroll=4)


def right_term(lg, eb, out):
    wd = 256

    def part(t, _):
        cols = pl.ds(pl.multiple_of(t * wd, wd), wd)
        v = jnp.dot(lg[...], eb[:, cols], preferred_element_type=F32)
        out[:, :, cols] = v.reshape(16, 16, wd).astype(BF)
        return 0

    lax.fori_loop(0, 512 // wd, part, 0, unroll=2)


def outer_weight(half, lg, rg, gt, out):
    wd = 512
    o = lax.dot_general(
        lg[:, half * wd : half * wd + wd], rg[...], (((0,), (0,)), ((), ())), preferred_element_type=F32
    )
    o = (o * (1.0 / 256)).astype(BF)
    tiles = []
    for h in range(wd // 128):
        parts = [[None] * 2 for _ in range(16)]
        for jg in range(4):
            for i0 in range(2):
                x = []
                for q in range(4):
                    r0 = h * 128 + q * 32 + 16 * i0
                    x.append(o[r0 : r0 + 16, 128 * jg : 128 * jg + 128])
                y = swap4(x)
                for b in range(4):
                    parts[4 * jg + b][i0] = y[b]
        tiles.append(jnp.concatenate([p for q in parts for p in q], axis=0))
    v = jnp.dot(gt[...], jnp.concatenate(tiles, axis=1), preferred_element_type=F32).T
    out[half * 16 : half * 16 + 16] = v.reshape(16, 32, 128).astype(BF)


def kernel(
    l_hbm, r_hbm, g_hbm, w_hbm, lo, ro, wo,
    lv, rv, gv, wv, lf, rf, gf, lflat, rflat, gji, gt,
    lb, rb, lg, rg, eb,
    sl, ra, sa, sb, rl, sr, rr, sw, rw, zb, ab,
    in_sem, ag_l, ag_r, rs_a, rs_b, rs_r, rs_w, z_w, ag_w,
):
    row, col = lax.axis_index("row"), lax.axis_index("col")
    z, xl = col // XL, col % XL
    plane = xl * ROWS + row

    def at_zx(dz, dx):
        c = ((z + dz) % ZS) * XL + (xl + dx) % XL
        return {"row": row, "col": c}

    def row_at(k):
        r = (row + k) % ROWS
        return {"row": r, "col": col}, r

    def plane_at(k):
        r, x = (row + k % ROWS) % ROWS, (xl + k // ROWS) % XL
        return {"row": r, "col": z * XL + x}, x * ROWS + r

    def z_at(k):
        zz = (z + k) % ZS
        return {"row": row, "col": zz * XL + xl}, zz

    inputs = [
        pltpu.make_async_copy(src, dst, in_sem.at[n])
        for n, (src, dst) in enumerate(((l_hbm, lv), (r_hbm, rv), (g_hbm, gv), (w_hbm, wv)))
    ]
    for c in inputs:
        c.start()

    barrier = pltpu.get_barrier_semaphore()

    def greet(device):
        pl.semaphore_signal(barrier, inc=1, device_id=device, device_id_type=MESH)

    def greet_all(at, first, last):
        def one(k, _):
            greet(at(k)[0])
            return 0

        lax.fori_loop(first, last, one, 0)

    greet(at_zx(4, 0))
    greet(at_zx(-4, 0))
    greet_all(row_at, 1, ROWS)
    for dz, dx in NEAR:
        greet(at_zx(-dz, dx))
    greet_all(plane_at, ROWS + 1, PLANE)

    inputs[0].wait()
    inputs[1].wait()
    lf[...] = jnp.swapaxes(lv[...].astype(F32), 1, 2).reshape(256, 32)
    rf[...] = rv[...].reshape(256, 32).astype(F32)
    for i in range(32):
        lflat[:, 32 * i : 32 * i + 32] = lf[pl.ds(i, 8, stride=32), :]
    for j in range(16):
        rflat[:, 32 * j : 32 * j + 32] = rf[pl.ds(j, 16, stride=16), :]
    lb[col] = lflat[...].astype(BF)
    rb[row] = rflat[...].astype(BF)

    pl.semaphore_wait(barrier, GREETED)

    def left_copy(d, dz, dx):
        slot = ((z + ZS - d) % ZS) * XL + xl
        k = ((d + dz) % ZS) * XL + dx
        return pltpu.make_async_remote_copy(
            src_ref=lb.at[slot],
            dst_ref=lb.at[slot],
            send_sem=ag_l.at[0, k],
            recv_sem=ag_l.at[1, k],
            device_id=at_zx(dz, dx),
            device_id_type=MESH,
        )

    def left_arrived(k, wait):
        slot = ((z + ZS - k // XL) % ZS) * XL + (xl + k % XL) % XL
        c = pltpu.make_async_remote_copy(
            src_ref=lb.at[slot],
            dst_ref=lb.at[slot],
            send_sem=ag_l.at[0, k],
            recv_sem=ag_l.at[1, k],
            device_id=at_zx(0, 1),
            device_id_type=MESH,
        )
        wait(c)

    def spread(d):
        for dz, dx in NEAR:
            left_copy(d, dz, dx).start()

    def copies(at, n, src_slot, dst_slot, sems):
        def make(k):
            where, slot = at(k)
            return pltpu.make_async_remote_copy(
                src_ref=src_slot(slot),
                dst_ref=dst_slot,
                send_sem=sems.at[0, k],
                recv_sem=sems.at[1, k],
                device_id=where,
                device_id_type=MESH,
            )

        def each(act, first, last):
            def one(k, _):
                act(make(k))
                return 0

            lax.fori_loop(first, last, one, 0)

        return (
            lambda first=1, last=n: each(lambda c: c.start(), first, last),
            lambda: each(lambda c: c.wait_recv(), 1, n),
            lambda: each(lambda c: c.wait_send(), 1, n),
        )

    ag_r_start, ag_r_recv, ag_r_sent = copies(row_at, ROWS, lambda s: rb.at[row], rb.at[row], ag_r)
    rs_r_start, rs_r_recv, rs_r_sent = copies(row_at, ROWS, lambda s: sr.at[s], rr.at[row], rs_r)
    rs_w_start, rs_w_recv, rs_w_sent = copies(plane_at, PLANE, lambda s: sw.at[s], rw.at[plane], rs_w)
    z_w_start, z_w_recv, z_w_sent = copies(z_at, ZS, lambda s: zb.at[z], zb.at[z], z_w)
    ag_w_start, ag_w_recv, ag_w_sent = copies(plane_at, PLANE, lambda s: ab.at[plane], ab.at[plane], ag_w)

    left_copy(0, 4, 0).start()
    left_copy(0, -4, 0).start()
    ag_r_start()
    spread(0)

    inputs[2].wait()
    inputs[3].wait()
    gf[...] = gv[...].reshape(512, 128).astype(F32)
    for j in range(16):
        gji[32 * j : 32 * j + 32, :] = gf[pl.ds(j, 32, stride=16), :].astype(BF)
    gt[...] = gji[...].T
    expand(gji, wv, eb)

    left_arrived(4 * XL, lambda c: c.wait_recv())
    left_copy(4, 4, 0).start()
    spread(4)
    left_arrived(12 * XL, lambda c: c.wait_recv())
    spread(12)
    ag_r_recv()
    rg[...] = rb[...].reshape(256, 512)
    left_term(rg, eb, sl)
    left_arrived(8 * XL, lambda c: c.wait_recv())
    spread(8)

    zr, zq = z % 4, z // 4

    def group_copy(n):
        dz, dx = NEAR[n]
        return pltpu.make_async_remote_copy(
            src_ref=sl.at[(z + dz) % 4, (xl + dx) % XL],
            dst_ref=ra.at[n],
            send_sem=rs_a.at[0, n],
            recv_sem=rs_a.at[1, n],
            device_id=at_zx(dz, dx),
            device_id_type=MESH,
        )

    for n in range(len(NEAR)):
        group_copy(n).start()

    def rest(act):
        def one(k, _):
            left_arrived(k, act)
            return 0

        lax.fori_loop(1, 8, one, 0)
        lax.fori_loop(9, 16, one, 0)
        lax.fori_loop(17, 24, one, 0)
        lax.fori_loop(25, 32, one, 0)

    rest(lambda c: c.wait_recv())
    lg[...] = lb[...].astype(F32).reshape(256, 1024).astype(BF)
    for half in range(2):
        outer_weight(half, lg, rg, gt, sw)
        away = (xl + half) % XL
        rs_w_start(away * ROWS + (1 - away), away * ROWS + ROWS)
    rw[plane] = sw[plane]
    right_term(lg, eb, sr)
    rs_r_start()
    rr[row] = sr[row]

    for n in range(len(NEAR)):
        group_copy(n).wait_recv()
    v = sl[zr, xl].astype(F32)
    for n in range(len(NEAR)):
        v = v + ra[n].astype(F32)
    sa[...] = v
    sb[...] = v.astype(BF)

    def far_copy(q):
        return pltpu.make_async_remote_copy(
            src_ref=sb.at[(zq + q) % 4],
            dst_ref=rl.at[q - 1],
            send_sem=rs_b.at[0, q],
            recv_sem=rs_b.at[1, q],
            device_id=at_zx(4 * q, 0),
            device_id_type=MESH,
        )

    for q in (2, 1, 3):
        far_copy(q).start()

    rs_w_recv()
    zb[z] = jnp.sum(rw[...].astype(F32), axis=0).astype(BF)
    z_w_start()
    rs_r_recv()
    rflat[...] = jnp.sum(rr[...].astype(F32), axis=0)
    for j in range(16):
        ro[:, j, :] = rflat[:, 32 * j : 32 * j + 32]
    z_w_recv()
    ab[plane] = jnp.sum(zb[...].astype(F32), axis=0).astype(BF)
    ag_w_start()
    for q in (1, 2, 3):
        far_copy(q).wait_recv()
    lflat[...] = sa[zq] + rl[0].astype(F32) + rl[1].astype(F32) + rl[2].astype(F32)
    for i in range(32):
        lf[pl.ds(i, 8, stride=32), :] = lflat[:, 32 * i : 32 * i + 32]
    lo[...] = jnp.swapaxes(lf[...].reshape(8, 32, 32), 1, 2)
    ag_w_recv()
    wo[...] = ab[...].astype(F32).reshape(1024, 128) * (1.0 / 512)

    for done in (ag_r_sent, rs_r_sent, rs_w_sent, z_w_sent, ag_w_sent):
        done()
    rest(lambda c: c.wait_send())
    for d in (4, 8, 12):
        left_arrived(d * XL, lambda c: c.wait_send())
    for n in range(len(NEAR)):
        group_copy(n).wait_send()
    for q in (1, 2, 3):
        far_copy(q).wait_send()


def per_device(left_panel, right_panel, pair_grad, out_weight):
    V = pltpu.VMEM
    dma = pltpu.SemaphoreType.DMA
    return pl.pallas_call(
        kernel,
        out_shape=[
            jax.ShapeDtypeStruct((8, 32, 32), F32),
            jax.ShapeDtypeStruct((16, 16, 32), F32),
            jax.ShapeDtypeStruct((1024, 128), F32),
        ],
        in_specs=[pl.BlockSpec(memory_space=pltpu.HBM)] * 4,
        out_specs=[pl.BlockSpec(memory_space=V)] * 3,
        scratch_shapes=[
            V((8, 32, 32), BF), V((16, 16, 32), BF), V((32, 16, 128), BF), V((1024, 128), BF),
            V((256, 32), F32), V((256, 32), F32), V((512, 128), F32),
            V((8, 1024), F32), V((16, 512), F32), V((512, 128), BF), V((128, 512), BF),
            V((32, 8, 1024), BF), V((16, 16, 512), BF), V((256, 1024), BF), V((256, 512), BF), V((1024, 512), BF),
            V((4, 2, 4, 8, 1024), BF), V((7, 4, 8, 1024), BF), V((4, 8, 1024), F32), V((4, 8, 1024), BF), V((3, 8, 1024), BF),
            V((16, 16, 512), BF), V((16, 16, 512), BF),
            V((32, 32, 128), BF), V((32, 32, 128), BF), V((16, 32, 128), BF), V((32, 32, 128), BF),
            dma((4,)), dma((2, 32)), dma((2, 16)), dma((2, 7)), dma((2, 4)), dma((2, 16)), dma((2, 32)), dma((2, 16)), dma((2, 32)),
        ],
        compiler_params=pltpu.CompilerParams(
            collective_id=0, has_side_effects=True, vmem_limit_bytes=60 << 20
        ),
        cost_estimate=pl.CostEstimate(flops=1 << 30, bytes_accessed=1 << 20, transcendentals=0),
        name="pair_backward",
    )(left_panel, right_panel, pair_grad, out_weight)


def solution(mesh):
    in_specs = (P("col", "row", None), P("row", "col", None), P("row", "col", None), P())
    out_specs = (P("col", "row", None), P("row", "col", None), P())
    return jax.shard_map(
        per_device, mesh=mesh, in_specs=in_specs, out_specs=out_specs, check_vma=False
    )
```

```python
import jax
import jax.numpy as jnp
from jax import lax
from jax.experimental import pallas as pl
from jax.experimental.pallas import tpu as pltpu
from jax.sharding import PartitionSpec as P

MESH = pl.DeviceIdType.MESH
F32, BF = jnp.float32, jnp.bfloat16
ROWS, ZS, XL = 16, 16, 2
COLS = ZS * XL
PLANE = ROWS * XL
NEAR = ((2, 0), (2, 1), (1, 1), (-1, 1), (1, 0), (-1, 0), (0, 1))
GREETED = len(NEAR) + 2 + (ROWS - 1)


def swap4(x):
    lane = lax.broadcasted_iota(jnp.int32, x[0].shape, 1)
    low = lane < 64
    even = (lane // 32) % 2 == 0
    r = [pltpu.roll(v, 64, 1) for v in x]
    a = [
        jnp.where(low, x[0], r[2]),
        jnp.where(low, x[1], r[3]),
        jnp.where(low, r[0], x[2]),
        jnp.where(low, r[1], x[3]),
    ]
    y = []
    for p in (0, 2):
        y.append(jnp.where(even, a[p], pltpu.roll(a[p + 1], 32, 1)))
        y.append(jnp.where(even, pltpu.roll(a[p], 96, 1), a[p + 1]))
    return y


def expand(gji, w, eb):
    wd = 256

    def part(a, _):
        w_rows = w[pl.ds(pl.multiple_of(a * wd, wd), wd), :]
        m = lax.dot_general(gji[...], w_rows, (((1,), (1,)), ((), ())), preferred_element_type=F32)
        m = (m * (1.0 / 256)).astype(BF)
        for h in range(wd // 128):
            for jg in range(4):
                for i0 in range(2):
                    x = []
                    for b in range(4):
                        r0 = (4 * jg + b) * 32 + 16 * i0
                        x.append(m[r0 : r0 + 16, 128 * h : 128 * h + 128])
                    y = swap4(x)
                    for q in range(4):
                        r0 = pl.multiple_of(a * wd + h * 128 + q * 32 + 16 * i0, 16)
                        eb[pl.ds(r0, 16), 128 * jg : 128 * jg + 128] = y[q]
        return 0

    lax.fori_loop(0, 1024 // wd, part, 0, unroll=4)


def left_term(rg, eb, out):
    wd = 256

    def part(t, _):
        rows = pl.ds(pl.multiple_of(t * wd, wd), wd)
        v = lax.dot_general(rg[...], eb[rows, :], (((1,), (1,)), ((), ())), preferred_element_type=F32)
        for m in range(4):
            out[:, :, m, :, rows] = v[64 * m : 64 * m + 64].reshape(4, 2, 8, wd).astype(BF)
        return 0

    lax.fori_loop(0, 1024 // wd, part, 0, unroll=4)


def right_term(lg, eb, out):
    wd = 256

    def part(t, _):
        cols = pl.ds(pl.multiple_of(t * wd, wd), wd)
        v = jnp.dot(lg[...], eb[:, cols], preferred_element_type=F32)
        out[:, :, cols] = v.reshape(16, 16, wd).astype(BF)
        return 0

    lax.fori_loop(0, 512 // wd, part, 0, unroll=2)


def outer_weight(half, lg, rg, gt, out):
    wd = 512
    o = lax.dot_general(
        lg[:, pl.ds(pl.multiple_of(half * wd, wd), wd)], rg[...], (((0,), (0,)), ((), ())), preferred_element_type=F32
    )
    o = (o * (1.0 / 256)).astype(BF)
    tiles = []
    for h in range(wd // 128):
        parts = [[None] * 2 for _ in range(16)]
        for jg in range(4):
            for i0 in range(2):
                x = []
                for q in range(4):
                    r0 = h * 128 + q * 32 + 16 * i0
                    x.append(o[r0 : r0 + 16, 128 * jg : 128 * jg + 128])
                y = swap4(x)
                for b in range(4):
                    parts[4 * jg + b][i0] = y[b]
        tiles.append(jnp.concatenate([p for q in parts for p in q], axis=0))
    v = jnp.dot(gt[...], jnp.concatenate(tiles, axis=1), preferred_element_type=F32).T
    out[pl.ds(half * 16, 16)] = v.reshape(16, 32, 128).astype(BF)


def kernel(
    l_hbm, r_hbm, g_hbm, w_hbm, lo, ro, wo,
    lv, rv, gv, wv, lf, rf, gf, lflat, rflat, gji, gt,
    lb, rb, lg, rg, eb,
    sl, ra, sa, sb, rl, sr, rr, sw, rw, zb, ab,
    in_sem, ag_l, ag_r, rs_a, rs_b, rs_r, rs_w, z_w, ag_w,
):
    row, col = lax.axis_index("row"), lax.axis_index("col")
    z, xl = col // XL, col % XL
    plane = xl * ROWS + row

    def at_zx(dz, dx):
        c = ((z + dz) % ZS) * XL + (xl + dx) % XL
        return {"row": row, "col": c}

    def row_at(k):
        r = (row + k) % ROWS
        return {"row": r, "col": col}, r

    def plane_at(k):
        r, x = (row + k % ROWS) % ROWS, (xl + k // ROWS) % XL
        return {"row": r, "col": z * XL + x}, x * ROWS + r

    def z_at(k):
        zz = (z + ZS // 2 + k // 2 * (1 - 2 * (1 - k % 2))) % ZS
        return {"row": row, "col": zz * XL + xl}, zz

    inputs = [
        pltpu.make_async_copy(src, dst, in_sem.at[n])
        for n, (src, dst) in enumerate(((l_hbm, lv), (r_hbm, rv), (g_hbm, gv), (w_hbm, wv)))
    ]
    for c in inputs:
        c.start()

    barrier = pltpu.get_barrier_semaphore()

    def greet(device):
        pl.semaphore_signal(barrier, inc=1, device_id=device, device_id_type=MESH)

    def greet_all(at, first, last):
        def one(k, _):
            greet(at(k)[0])
            return 0

        lax.fori_loop(first, last, one, 0)

    greet(at_zx(4, 0))
    greet(at_zx(-4, 0))
    greet_all(row_at, 1, ROWS)
    for dz, dx in NEAR:
        greet(at_zx(-dz, dx))

    inputs[0].wait()
    inputs[1].wait()
    lf[...] = jnp.swapaxes(lv[...].astype(F32), 1, 2).reshape(256, 32)
    rf[...] = rv[...].reshape(256, 32).astype(F32)
    for i in range(32):
        lflat[:, 32 * i : 32 * i + 32] = lf[pl.ds(i, 8, stride=32), :]
    for j in range(16):
        rflat[:, 32 * j : 32 * j + 32] = rf[pl.ds(j, 16, stride=16), :]
    lb[col] = lflat[...].astype(BF)
    rb[row] = rflat[...].astype(BF)

    pl.semaphore_wait(barrier, GREETED)

    def left_copy(d, dz, dx):
        slot = ((z + ZS - d) % ZS) * XL + xl
        k = ((d + dz) % ZS) * XL + dx
        return pltpu.make_async_remote_copy(
            src_ref=lb.at[slot],
            dst_ref=lb.at[slot],
            send_sem=ag_l.at[0, k],
            recv_sem=ag_l.at[1, k],
            device_id=at_zx(dz, dx),
            device_id_type=MESH,
        )

    def left_arrived(k, wait):
        slot = ((z + ZS - k // XL) % ZS) * XL + (xl + k % XL) % XL
        c = pltpu.make_async_remote_copy(
            src_ref=lb.at[slot],
            dst_ref=lb.at[slot],
            send_sem=ag_l.at[0, k],
            recv_sem=ag_l.at[1, k],
            device_id=at_zx(0, 1),
            device_id_type=MESH,
        )
        wait(c)

    def spread(d):
        for dz, dx in NEAR:
            left_copy(d, dz, dx).start()

    def copies(at, n, src_slot, dst_slot, sems):
        def make(k):
            where, slot = at(k)
            return pltpu.make_async_remote_copy(
                src_ref=src_slot(slot),
                dst_ref=dst_slot,
                send_sem=sems.at[0, k],
                recv_sem=sems.at[1, k],
                device_id=where,
                device_id_type=MESH,
            )

        def each(act, first, last):
            def one(k, _):
                act(make(k))
                return 0

            lax.fori_loop(first, last, one, 0)

        return (
            lambda first=1, last=n: each(lambda c: c.start(), first, last),
            lambda: each(lambda c: c.wait_recv(), 1, n),
            lambda: each(lambda c: c.wait_send(), 1, n),
        )

    ag_r_start, ag_r_recv, ag_r_sent = copies(row_at, ROWS, lambda s: rb.at[row], rb.at[row], ag_r)
    rs_r_start, rs_r_recv, rs_r_sent = copies(row_at, ROWS, lambda s: sr.at[s], rr.at[row], rs_r)
    rs_w_start, rs_w_recv, rs_w_sent = copies(plane_at, PLANE, lambda s: sw.at[s], rw.at[plane], rs_w)
    z_w_start, z_w_recv, z_w_sent = copies(z_at, ZS, lambda s: zb.at[z], zb.at[z], z_w)
    ag_w_start, ag_w_recv, ag_w_sent = copies(plane_at, PLANE, lambda s: ab.at[plane], ab.at[plane], ag_w)

    left_copy(0, 4, 0).start()
    left_copy(0, -4, 0).start()
    ag_r_start()
    spread(0)

    inputs[2].wait()
    inputs[3].wait()
    gf[...] = gv[...].reshape(512, 128).astype(F32)
    for j in range(16):
        gji[32 * j : 32 * j + 32, :] = gf[pl.ds(j, 32, stride=16), :].astype(BF)
    gt[...] = gji[...].T
    expand(gji, wv, eb)

    left_arrived(4 * XL, lambda c: c.wait_recv())
    left_copy(4, 4, 0).start()
    spread(4)
    left_arrived(12 * XL, lambda c: c.wait_recv())
    spread(12)
    left_arrived(8 * XL, lambda c: c.wait_recv())
    spread(8)
    ag_r_recv()
    rg[...] = rb[...].reshape(256, 512)
    left_term(rg, eb, sl)

    zr, zq = z % 4, z // 4

    def group_copy(n):
        dz, dx = NEAR[n]
        return pltpu.make_async_remote_copy(
            src_ref=sl.at[(z + dz) % 4, (xl + dx) % XL],
            dst_ref=ra.at[n],
            send_sem=rs_a.at[0, n],
            recv_sem=rs_a.at[1, n],
            device_id=at_zx(dz, dx),
            device_id_type=MESH,
        )

    for n in range(len(NEAR)):
        group_copy(n).start()

    def rest(act):
        def one(k, _):
            left_arrived(k, act)
            return 0

        lax.fori_loop(1, 8, one, 0)
        lax.fori_loop(9, 16, one, 0)
        lax.fori_loop(17, 24, one, 0)
        lax.fori_loop(25, 32, one, 0)

    rest(lambda c: c.wait_recv())
    lg[...] = lb[...].astype(F32).reshape(256, 1024).astype(BF)
    outer_weight(1 - xl, lg, rg, gt, sw)
    rs_w_start(ROWS, PLANE)
    outer_weight(xl, lg, rg, gt, sw)
    rs_w_start(1, ROWS)
    rw[plane] = sw[plane]
    right_term(lg, eb, sr)
    rs_r_start()
    rr[row] = sr[row]

    for n in range(len(NEAR)):
        group_copy(n).wait_recv()
    v = sl[zr, xl].astype(F32)
    for n in range(len(NEAR)):
        v = v + ra[n].astype(F32)
    sa[...] = v
    sb[...] = v.astype(BF)

    def far_copy(q):
        return pltpu.make_async_remote_copy(
            src_ref=sb.at[(zq + q) % 4],
            dst_ref=rl.at[q - 1],
            send_sem=rs_b.at[0, q],
            recv_sem=rs_b.at[1, q],
            device_id=at_zx(4 * q, 0),
            device_id_type=MESH,
        )

    for q in (2, 1, 3):
        far_copy(q).start()

    rs_w_recv()
    zb[z] = jnp.sum(rw[...].astype(F32), axis=0).astype(BF)
    z_w_start()
    rs_r_recv()
    rflat[...] = jnp.sum(rr[...].astype(F32), axis=0)
    for j in range(16):
        ro[:, j, :] = rflat[:, 32 * j : 32 * j + 32]
    z_w_recv()
    ab[plane] = jnp.sum(zb[...].astype(F32), axis=0).astype(BF)
    ag_w_start()
    for q in (1, 2, 3):
        far_copy(q).wait_recv()
    lflat[...] = sa[zq] + rl[0].astype(F32) + rl[1].astype(F32) + rl[2].astype(F32)
    for i in range(32):
        lf[pl.ds(i, 8, stride=32), :] = lflat[:, 32 * i : 32 * i + 32]
    lo[...] = jnp.swapaxes(lf[...].reshape(8, 32, 32), 1, 2)
    ag_w_recv()
    wo[...] = ab[...].astype(F32).reshape(1024, 128) * (1.0 / 512)

    for done in (ag_r_sent, rs_r_sent, rs_w_sent, z_w_sent, ag_w_sent):
        done()
    rest(lambda c: c.wait_send())
    for d in (4, 8, 12):
        left_arrived(d * XL, lambda c: c.wait_send())
    for n in range(len(NEAR)):
        group_copy(n).wait_send()
    for q in (1, 2, 3):
        far_copy(q).wait_send()


def hand_over(l, r, w, lo, ro, wo, sem):
    moves = [pltpu.make_async_copy(a, b, sem.at[n]) for n, (a, b) in enumerate(((w, wo), (l, lo), (r, ro)))]
    for m in moves:
        m.start()
    for m in moves:
        m.wait()


def per_device(left_panel, right_panel, pair_grad, out_weight):
    V = pltpu.VMEM
    dma = pltpu.SemaphoreType.DMA
    args = [pltpu.with_memory_space_constraint(a, pltpu.HBM) for a in (left_panel, right_panel, pair_grad, out_weight)]
    raw = pl.pallas_call(
        kernel,
        out_shape=[
            jax.ShapeDtypeStruct((8, 32, 32), F32),
            jax.ShapeDtypeStruct((16, 16, 32), F32),
            jax.ShapeDtypeStruct((1024, 128), F32),
        ],
        in_specs=[pl.BlockSpec(memory_space=pltpu.HBM)] * 4,
        out_specs=[pl.BlockSpec(memory_space=V)] * 3,
        scratch_shapes=[
            V((8, 32, 32), BF), V((16, 16, 32), BF), V((32, 16, 128), BF), V((1024, 128), BF),
            V((256, 32), F32), V((256, 32), F32), V((512, 128), F32),
            V((8, 1024), F32), V((16, 512), F32), V((512, 128), BF), V((128, 512), BF),
            V((32, 8, 1024), BF), V((16, 16, 512), BF), V((256, 1024), BF), V((256, 512), BF), V((1024, 512), BF),
            V((4, 2, 4, 8, 1024), BF), V((7, 4, 8, 1024), BF), V((4, 8, 1024), F32), V((4, 8, 1024), BF), V((3, 8, 1024), BF),
            V((16, 16, 512), BF), V((16, 16, 512), BF),
            V((32, 32, 128), BF), V((32, 32, 128), BF), V((16, 32, 128), BF), V((32, 32, 128), BF),
            dma((4,)), dma((2, 32)), dma((2, 16)), dma((2, 7)), dma((2, 4)), dma((2, 16)), dma((2, 32)), dma((2, 16)), dma((2, 32)),
        ],
        compiler_params=pltpu.CompilerParams(
            collective_id=0, has_side_effects=True, vmem_limit_bytes=24 << 20
        ),
        cost_estimate=pl.CostEstimate(flops=1 << 30, bytes_accessed=1 << 20, transcendentals=0),
        name="pair_backward",
    )(*args)
    shapes = [jax.ShapeDtypeStruct(a.shape, a.dtype) for a in raw]
    return pl.pallas_call(
        hand_over,
        out_shape=shapes,
        in_specs=[pl.BlockSpec(memory_space=V)] * 3,
        out_specs=[pl.BlockSpec(memory_space=pltpu.HBM)] * 3,
        scratch_shapes=[dma((3,))],
        name="hand_over",
    )(*[pltpu.with_memory_space_constraint(a, V) for a in raw])


def solution(mesh):
    in_specs = (P("col", "row", None), P("row", "col", None), P("row", "col", None), P())
    out_specs = (P("col", "row", None), P("row", "col", None), P())
    return jax.shard_map(
        per_device, mesh=mesh, in_specs=in_specs, out_specs=out_specs, check_vma=False
    )
```

```python
import jax
import jax.numpy as jnp
from jax import lax
from jax.experimental import pallas as pl
from jax.experimental.pallas import tpu as pltpu
from jax.sharding import PartitionSpec as P

MESH = pl.DeviceIdType.MESH
F32, BF = jnp.float32, jnp.bfloat16
ROWS, ZS, XL = 16, 16, 2
COLS = ZS * XL
CHIPS = 16
NEAR = ((2, 1), (-2, 1), (2, 0), (-2, 0), (1, 1), (-1, 1), (1, 0), (-1, 0), (0, 1))
FAR = 5
LAST = ((3, 1), (3, 0))
GREETED = len(NEAR) + 2 + len(LAST) + (ROWS - 1)
GROUP = ((2, 1), (2, 0), (1, 1), (-1, 1), (1, 0), (-1, 0), (0, 1))
ACROSS = (6, 5, 7, 10, 14, 2, 4, 9, 11, 13, 15, 1, 3, 8, 12)


def swap4(x):
    lane = lax.broadcasted_iota(jnp.int32, x[0].shape, 1)
    low = lane < 64
    even = (lane // 32) % 2 == 0
    r = [pltpu.roll(v, 64, 1) for v in x]
    a = [
        jnp.where(low, x[0], r[2]),
        jnp.where(low, x[1], r[3]),
        jnp.where(low, r[0], x[2]),
        jnp.where(low, r[1], x[3]),
    ]
    y = []
    for p in (0, 2):
        y.append(jnp.where(even, a[p], pltpu.roll(a[p + 1], 32, 1)))
        y.append(jnp.where(even, pltpu.roll(a[p], 96, 1), a[p + 1]))
    return y


def expand(gji, w, eb):
    wd = 256

    def part(a, _):
        w_rows = w[pl.ds(pl.multiple_of(a * wd, wd), wd), :]
        m = lax.dot_general(gji[...], w_rows, (((1,), (1,)), ((), ())), preferred_element_type=F32)
        m = (m * (1.0 / 256)).astype(BF)
        for h in range(wd // 128):
            for jg in range(4):
                for i0 in range(2):
                    x = []
                    for b in range(4):
                        r0 = (4 * jg + b) * 32 + 16 * i0
                        x.append(m[r0 : r0 + 16, 128 * h : 128 * h + 128])
                    y = swap4(x)
                    for q in range(4):
                        r0 = pl.multiple_of(a * wd + h * 128 + q * 32 + 16 * i0, 16)
                        eb[pl.ds(r0, 16), 128 * jg : 128 * jg + 128] = y[q]
        return 0

    lax.fori_loop(0, 1024 // wd, part, 0, unroll=4)


def left_term(rg, eb, out):
    wd = 256

    def part(t, _):
        rows = pl.ds(pl.multiple_of(t * wd, wd), wd)
        v = lax.dot_general(rg[...], eb[rows, :], (((1,), (1,)), ((), ())), preferred_element_type=F32)
        for m in range(4):
            out[:, :, m, :, rows] = v[64 * m : 64 * m + 64].reshape(4, 2, 8, wd).astype(BF)
        return 0

    lax.fori_loop(0, 1024 // wd, part, 0, unroll=4)


def right_term(lg, eb, out):
    wd = 256

    def part(t, _):
        cols = pl.ds(pl.multiple_of(t * wd, wd), wd)
        v = jnp.dot(lg[...], eb[:, cols], preferred_element_type=F32)
        out[:, :, cols] = v.reshape(16, 16, wd).astype(BF)
        return 0

    lax.fori_loop(0, 512 // wd, part, 0, unroll=2)


def outer_weight(half, lg, rg, gt):
    wd = 512
    o = lax.dot_general(
        lg[:, pl.ds(pl.multiple_of(half * wd, wd), wd)], rg[...], (((0,), (0,)), ((), ())), preferred_element_type=F32
    )
    o = (o * (1.0 / 256)).astype(BF)
    tiles = []
    for h in range(wd // 128):
        parts = [[None] * 2 for _ in range(16)]
        for jg in range(4):
            for i0 in range(2):
                x = []
                for q in range(4):
                    r0 = h * 128 + q * 32 + 16 * i0
                    x.append(o[r0 : r0 + 16, 128 * jg : 128 * jg + 128])
                y = swap4(x)
                for b in range(4):
                    parts[4 * jg + b][i0] = y[b]
        tiles.append(jnp.concatenate([p for q in parts for p in q], axis=0))
    v = jnp.dot(gt[...], jnp.concatenate(tiles, axis=1), preferred_element_type=F32).T
    return v.reshape(16, 32, 128)


def kernel(
    l_hbm, r_hbm, g_hbm, w_hbm, lo, ro, wo,
    lv, rv, gv, wv, lf, rf, gf, lflat, rflat, gji, gt,
    lb, rb, lg, rg, eb,
    sl, ra, sa, sb, rl, sr, rr, wp, wq, sw, rw, zb, ab,
    in_sem, ag_l, ag_r, rs_a, rs_b, rs_r, c_w, rs_w, z_w, ag_w, f_w,
):
    row, col = lax.axis_index("row"), lax.axis_index("col")
    z, xl = col // XL, col % XL
    xh, y, core = row // 8, (row // 2) % 4, row % 2
    chip = xl * 8 + row // 2
    partner = {"row": row + 1 - 2 * core, "col": col}

    def at_zx(dz, dx):
        c = ((z + dz) % ZS) * XL + (xl + dx) % XL
        return {"row": row, "col": c}

    def row_at(k):
        r = (row + k) % ROWS
        return {"row": r, "col": col}, r

    def chip_at(k, sign):
        r, x = ((xh + k // 4) % 2) * 4 + (y + sign * k) % 4, (xl + k // 8) % XL
        return {"row": r * 2 + core, "col": z * XL + x}, x * 8 + r

    def z_at(k):
        zz = (z + ZS // 2 + k // 2 * (1 - 2 * (1 - k % 2))) % ZS
        return {"row": row, "col": zz * XL + xl}, zz

    inputs = [
        pltpu.make_async_copy(src, dst, in_sem.at[n])
        for n, (src, dst) in enumerate(((l_hbm, lv), (r_hbm, rv), (g_hbm, gv), (w_hbm, wv)))
    ]
    for c in inputs:
        c.start()

    barrier = pltpu.get_barrier_semaphore()

    def greet(device):
        pl.semaphore_signal(barrier, inc=1, device_id=device, device_id_type=MESH)

    def greet_all(at, first, last):
        def one(k, _):
            greet(at(k)[0])
            return 0

        lax.fori_loop(first, last, one, 0)

    greet(at_zx(FAR, 0))
    greet(at_zx(-FAR, 0))
    greet_all(row_at, 1, ROWS)
    for dz, dx in LAST + NEAR:
        greet(at_zx(-dz, dx))

    inputs[0].wait()
    inputs[1].wait()
    lf[...] = jnp.swapaxes(lv[...].astype(F32), 1, 2).reshape(256, 32)
    rf[...] = rv[...].reshape(256, 32).astype(F32)
    for i in range(32):
        lflat[:, 32 * i : 32 * i + 32] = lf[pl.ds(i, 8, stride=32), :]
    for j in range(16):
        rflat[:, 32 * j : 32 * j + 32] = rf[pl.ds(j, 16, stride=16), :]
    lb[col] = lflat[...].astype(BF)
    rb[row] = rflat[...].astype(BF)

    pl.semaphore_wait(barrier, GREETED)

    def left_copy(d, dz, dx):
        slot = ((z + ZS - d) % ZS) * XL + xl
        k = ((d + dz) % ZS) * XL + dx
        return pltpu.make_async_remote_copy(
            src_ref=lb.at[slot],
            dst_ref=lb.at[slot],
            send_sem=ag_l.at[0, k],
            recv_sem=ag_l.at[1, k],
            device_id=at_zx(dz, dx),
            device_id_type=MESH,
        )

    def left_arrived(k, wait):
        slot = ((z + ZS - k // XL) % ZS) * XL + (xl + k % XL) % XL
        c = pltpu.make_async_remote_copy(
            src_ref=lb.at[slot],
            dst_ref=lb.at[slot],
            send_sem=ag_l.at[0, k],
            recv_sem=ag_l.at[1, k],
            device_id=at_zx(0, 1),
            device_id_type=MESH,
        )
        wait(c)

    def spread(d):
        for dz, dx in NEAR:
            left_copy(d, dz, dx).start()

    def copies(at, n, src_slot, dst_slot, sems):
        def make(k):
            where, slot = at(k)
            return pltpu.make_async_remote_copy(
                src_ref=src_slot(slot),
                dst_ref=dst_slot,
                send_sem=sems.at[0, k],
                recv_sem=sems.at[1, k],
                device_id=where,
                device_id_type=MESH,
            )

        def each(act, first, last):
            def one(k, _):
                act(make(k))
                return 0

            lax.fori_loop(first, last, one, 0)

        return (
            lambda first=1, last=n: each(lambda c: c.start(), first, last),
            lambda: each(lambda c: c.wait_recv(), 1, n),
            lambda: each(lambda c: c.wait_send(), 1, n),
        )

    ag_r_start, ag_r_recv, ag_r_sent = copies(row_at, ROWS, lambda s: rb.at[row], rb.at[row], ag_r)
    rs_r_start, rs_r_recv, rs_r_sent = copies(row_at, ROWS, lambda s: sr.at[s], rr.at[row], rs_r)
    z_w_start, z_w_recv, z_w_sent = copies(z_at, ZS, lambda s: zb.at[z], zb.at[z], z_w)

    left_copy(0, FAR, 0).start()
    left_copy(0, -FAR, 0).start()
    ag_r_start()
    spread(0)

    inputs[2].wait()
    inputs[3].wait()
    gf[...] = gv[...].reshape(512, 128).astype(F32)
    for j in range(16):
        gji[32 * j : 32 * j + 32, :] = gf[pl.ds(j, 32, stride=16), :].astype(BF)
    gt[...] = gji[...].T
    expand(gji, wv, eb)

    left_arrived(FAR * XL, lambda c: c.wait_recv())
    for dz, dx in LAST:
        left_copy(FAR, dz, dx).start()
    spread(FAR)
    left_arrived((ZS - FAR) * XL, lambda c: c.wait_recv())
    spread(ZS - FAR)
    ag_r_recv()
    rg[...] = rb[...].reshape(256, 512)
    left_term(rg, eb, sl)

    zr, zq = z % 4, z // 4

    def group_copy(n):
        dz, dx = GROUP[n]
        return pltpu.make_async_remote_copy(
            src_ref=sl.at[(z + dz) % 4, (xl + dx) % XL],
            dst_ref=ra.at[n],
            send_sem=rs_a.at[0, n],
            recv_sem=rs_a.at[1, n],
            device_id=at_zx(dz, dx),
            device_id_type=MESH,
        )

    def rest(act):
        def one(k, _):
            left_arrived(k, act)
            return 0

        lax.fori_loop(1, FAR * XL, one, 0)
        lax.fori_loop(FAR * XL + 1, (ZS - FAR) * XL, one, 0)
        lax.fori_loop((ZS - FAR) * XL + 1, COLS, one, 0)

    rest(lambda c: c.wait_recv())
    for n in range(len(GROUP)):
        group_copy(n).start()
    lg[...] = lb[...].astype(F32).reshape(256, 1024).astype(BF)
    halves = pltpu.make_async_remote_copy(
        src_ref=wp, dst_ref=wq, send_sem=c_w.at[0], recv_sem=c_w.at[1], device_id=partner, device_id_type=MESH
    )
    wp[...] = outer_weight(1 - core, lg, rg, gt)
    halves.start()
    own_half = outer_weight(core, lg, rg, gt)
    halves.wait_recv()
    sw[...] = (own_half + wq[...]).astype(BF)

    def share_copy(k):
        where, slot = chip_at(k, 1)
        return pltpu.make_async_remote_copy(
            src_ref=sw.at[slot],
            dst_ref=rw.at[chip],
            send_sem=rs_w.at[0, k],
            recv_sem=rs_w.at[1, k],
            device_id=where,
            device_id_type=MESH,
        )

    def back_copy(k):
        return pltpu.make_async_remote_copy(
            src_ref=ab.at[core, chip],
            dst_ref=ab.at[core, chip],
            send_sem=ag_w.at[0, k],
            recv_sem=ag_w.at[1, k],
            device_id=chip_at(k, 1)[0],
            device_id_type=MESH,
        )

    def pass_on(k):
        slot = chip_at(k, -1)[1]
        return pltpu.make_async_remote_copy(
            src_ref=ab.at[core, slot],
            dst_ref=ab.at[core, slot],
            send_sem=f_w.at[0, k],
            recv_sem=f_w.at[1, k],
            device_id=partner,
            device_id_type=MESH,
        )

    for k in ACROSS:
        share_copy(k).start()
    rw[chip] = sw[chip]
    right_term(lg, eb, sr)
    rr[row] = sr[row]
    for k in ACROSS:
        share_copy(k).wait_recv()
    zb[z] = jnp.sum(rw[...].astype(F32), axis=0).astype(BF)
    z_w_start()
    rs_r_start()

    for n in range(len(GROUP)):
        group_copy(n).wait_recv()
    v = sl[zr, xl].astype(F32)
    for n in range(len(GROUP)):
        v = v + ra[n].astype(F32)
    sa[...] = v
    sb[...] = v.astype(BF)

    def far_copy(q):
        return pltpu.make_async_remote_copy(
            src_ref=sb.at[(zq + q) % 4],
            dst_ref=rl.at[q - 1],
            send_sem=rs_b.at[0, q],
            recv_sem=rs_b.at[1, q],
            device_id=at_zx(4 * q, 0),
            device_id_type=MESH,
        )

    for q in (2, 1, 3):
        far_copy(q).start()

    z_w_recv()
    ab[core, chip] = jnp.sum(zb[...].astype(F32), axis=0).astype(BF)
    for k in ACROSS:
        back_copy(k).start()
    pass_on(0).start()
    rs_r_recv()
    rflat[...] = jnp.sum(rr[...].astype(F32), axis=0)
    for j in range(16):
        ro[:, j, :] = rflat[:, 32 * j : 32 * j + 32]
    for q in (1, 2, 3):
        far_copy(q).wait_recv()
    lflat[...] = sa[zq] + rl[0].astype(F32) + rl[1].astype(F32) + rl[2].astype(F32)
    for i in range(32):
        lf[pl.ds(i, 8, stride=32), :] = lflat[:, 32 * i : 32 * i + 32]
    lo[...] = jnp.swapaxes(lf[...].reshape(8, 32, 32), 1, 2)
    for k in ACROSS[::-1]:
        back_copy(k).wait_recv()
        pass_on(k).start()
    for k in range(CHIPS):
        pass_on(k).wait_recv()
    wo[...] = ab[...].astype(F32).reshape(1024, 128) * (1.0 / 512)

    for done in (ag_r_sent, rs_r_sent, z_w_sent):
        done()
    halves.wait_send()
    for k in ACROSS:
        share_copy(k).wait_send()
        back_copy(k).wait_send()
    for k in range(CHIPS):
        pass_on(k).wait_send()
    rest(lambda c: c.wait_send())
    for d in (FAR, ZS - FAR):
        left_arrived(d * XL, lambda c: c.wait_send())
    for n in range(len(GROUP)):
        group_copy(n).wait_send()
    for q in (1, 2, 3):
        far_copy(q).wait_send()


def hand_over(l, r, w, lo, ro, wo, sem):
    moves = [pltpu.make_async_copy(a, b, sem.at[n]) for n, (a, b) in enumerate(((w, wo), (l, lo), (r, ro)))]
    for m in moves:
        m.start()
    for m in moves:
        m.wait()


def per_device(left_panel, right_panel, pair_grad, out_weight):
    V = pltpu.VMEM
    dma = pltpu.SemaphoreType.DMA
    args = [pltpu.with_memory_space_constraint(a, pltpu.HBM) for a in (left_panel, right_panel, pair_grad, out_weight)]
    raw = pl.pallas_call(
        kernel,
        out_shape=[
            jax.ShapeDtypeStruct((8, 32, 32), F32),
            jax.ShapeDtypeStruct((16, 16, 32), F32),
            jax.ShapeDtypeStruct((1024, 128), F32),
        ],
        in_specs=[pl.BlockSpec(memory_space=pltpu.HBM)] * 4,
        out_specs=[pl.BlockSpec(memory_space=V)] * 3,
        scratch_shapes=[
            V((8, 32, 32), BF), V((16, 16, 32), BF), V((32, 16, 128), BF), V((1024, 128), BF),
            V((256, 32), F32), V((256, 32), F32), V((512, 128), F32),
            V((8, 1024), F32), V((16, 512), F32), V((512, 128), BF), V((128, 512), BF),
            V((32, 8, 1024), BF), V((16, 16, 512), BF), V((256, 1024), BF), V((256, 512), BF), V((1024, 512), BF),
            V((4, 2, 4, 8, 1024), BF), V((7, 4, 8, 1024), BF), V((4, 8, 1024), F32), V((4, 8, 1024), BF), V((3, 8, 1024), BF),
            V((16, 16, 512), BF), V((16, 16, 512), BF),
            V((16, 32, 128), F32), V((16, 32, 128), F32), V((16, 32, 128), BF), V((16, 32, 128), BF), V((16, 32, 128), BF), V((2, 16, 32, 128), BF),
            dma((4,)), dma((2, 32)), dma((2, 16)), dma((2, 7)), dma((2, 4)), dma((2, 16)),
            dma((2,)), dma((2, 16)), dma((2, 16)), dma((2, 16)), dma((2, 16)),
        ],
        compiler_params=pltpu.CompilerParams(
            collective_id=0, has_side_effects=True, vmem_limit_bytes=24 << 20
        ),
        cost_estimate=pl.CostEstimate(flops=1 << 30, bytes_accessed=1 << 20, transcendentals=0),
        name="pair_backward",
    )(*args)
    shapes = [jax.ShapeDtypeStruct(a.shape, a.dtype) for a in raw]
    return pl.pallas_call(
        hand_over,
        out_shape=shapes,
        in_specs=[pl.BlockSpec(memory_space=V)] * 3,
        out_specs=[pl.BlockSpec(memory_space=pltpu.HBM)] * 3,
        scratch_shapes=[dma((3,))],
        name="hand_over",
    )(*[pltpu.with_memory_space_constraint(a, V) for a in raw])


def solution(mesh):
    in_specs = (P("col", "row", None), P("row", "col", None), P("row", "col", None), P())
    out_specs = (P("col", "row", None), P("row", "col", None), P())
    return jax.shard_map(
        per_device, mesh=mesh, in_specs=in_specs, out_specs=out_specs, check_vma=False
    )
```

```python
import jax
import jax.numpy as jnp
from jax import lax
from jax.experimental import pallas as pl
from jax.experimental.pallas import tpu as pltpu
from jax.sharding import PartitionSpec as P

MESH = pl.DeviceIdType.MESH
F32, BF = jnp.float32, jnp.bfloat16
ROWS, ZS, XL = 16, 16, 2
COLS = ZS * XL
CHIPS = 16
NEAR = ((2, 1), (-2, 1), (2, 0), (-2, 0), (1, 1), (-1, 1), (1, 0), (-1, 0), (0, 1))
FAR = 5
LAST = ((3, 1), (3, 0))
GREETED = len(NEAR) + 2 + len(LAST) + (ROWS - 1)
GROUP = ((2, 1), (2, 0), (1, 1), (-1, 1), (1, 0), (-1, 0), (0, 1))
ACROSS = (6, 5, 7, 10, 14, 2, 4, 9, 11, 13, 15, 1, 3, 8, 12)


def swap4(x):
    lane = lax.broadcasted_iota(jnp.int32, x[0].shape, 1)
    low = lane < 64
    even = (lane // 32) % 2 == 0
    r = [pltpu.roll(v, 64, 1) for v in x]
    a = [
        jnp.where(low, x[0], r[2]),
        jnp.where(low, x[1], r[3]),
        jnp.where(low, r[0], x[2]),
        jnp.where(low, r[1], x[3]),
    ]
    y = []
    for p in (0, 2):
        y.append(jnp.where(even, a[p], pltpu.roll(a[p + 1], 32, 1)))
        y.append(jnp.where(even, pltpu.roll(a[p], 96, 1), a[p + 1]))
    return y


def expand(gji, w, eb):
    wd = 256

    def part(a, _):
        w_rows = w[pl.ds(pl.multiple_of(a * wd, wd), wd), :]
        m = lax.dot_general(gji[...], w_rows, (((1,), (1,)), ((), ())), preferred_element_type=F32)
        m = (m * (1.0 / 256)).astype(BF)
        for h in range(wd // 128):
            for jg in range(4):
                for i0 in range(2):
                    x = []
                    for b in range(4):
                        r0 = (4 * jg + b) * 32 + 16 * i0
                        x.append(m[r0 : r0 + 16, 128 * h : 128 * h + 128])
                    y = swap4(x)
                    for q in range(4):
                        r0 = pl.multiple_of(a * wd + h * 128 + q * 32 + 16 * i0, 16)
                        eb[pl.ds(r0, 16), 128 * jg : 128 * jg + 128] = y[q]
        return 0

    lax.fori_loop(0, 1024 // wd, part, 0, unroll=4)


def left_term(rg, eb, out):
    wd = 256

    def part(t, _):
        rows = pl.ds(pl.multiple_of(t * wd, wd), wd)
        v = lax.dot_general(rg[...], eb[rows, :], (((1,), (1,)), ((), ())), preferred_element_type=F32)
        for m in range(4):
            out[:, :, m, :, rows] = v[64 * m : 64 * m + 64].reshape(4, 2, 8, wd).astype(BF)
        return 0

    lax.fori_loop(0, 1024 // wd, part, 0, unroll=4)


def right_term(lg, eb, out):
    wd = 256

    def part(t, _):
        cols = pl.ds(pl.multiple_of(t * wd, wd), wd)
        v = jnp.dot(lg[...], eb[:, cols], preferred_element_type=F32)
        out[:, :, cols] = v.reshape(16, 16, wd).astype(BF)
        return 0

    lax.fori_loop(0, 512 // wd, part, 0, unroll=2)


def outer_weight(half, lg, rg, gt):
    wd = 512
    o = lax.dot_general(
        lg[:, pl.ds(pl.multiple_of(half * wd, wd), wd)], rg[...], (((0,), (0,)), ((), ())), preferred_element_type=F32
    )
    o = (o * (1.0 / 256)).astype(BF)
    tiles = []
    for h in range(wd // 128):
        parts = [[None] * 2 for _ in range(16)]
        for jg in range(4):
            for i0 in range(2):
                x = []
                for q in range(4):
                    r0 = h * 128 + q * 32 + 16 * i0
                    x.append(o[r0 : r0 + 16, 128 * jg : 128 * jg + 128])
                y = swap4(x)
                for b in range(4):
                    parts[4 * jg + b][i0] = y[b]
        tiles.append(jnp.concatenate([p for q in parts for p in q], axis=0))
    v = jnp.dot(gt[...], jnp.concatenate(tiles, axis=1), preferred_element_type=F32).T
    return v.reshape(16, 32, 128)


def kernel(
    l_hbm, r_hbm, g_hbm, w_hbm, lo, ro, wo,
    lv, rv, gv, wv, lf, rf, gf, lflat, rflat, gji, gt,
    lb, rb, lg, rg, eb,
    sl, ra, sa, sb, rl, sr, rr, wp, wq, sw, rw, zb, ab,
    in_sem, ag_l, ag_r, rs_a, rs_b, rs_r, c_w, rs_w, z_w, ag_w, f_w,
):
    row, col = lax.axis_index("row"), lax.axis_index("col")
    z, xl = col // XL, col % XL
    xh, y, core = row // 8, (row // 2) % 4, row % 2
    chip = xl * 8 + row // 2
    partner = {"row": row + 1 - 2 * core, "col": col}

    def at_zx(dz, dx):
        c = ((z + dz) % ZS) * XL + (xl + dx) % XL
        return {"row": row, "col": c}

    def row_at(k):
        r = (row + k) % ROWS
        return {"row": r, "col": col}, r

    def chip_at(k, sign):
        r, x = ((xh + k // 4) % 2) * 4 + (y + sign * k) % 4, (xl + k // 8) % XL
        return {"row": r * 2 + core, "col": z * XL + x}, x * 8 + r

    def z_at(k):
        zz = (z + ZS // 2 + k // 2 * (1 - 2 * (1 - k % 2))) % ZS
        return {"row": row, "col": zz * XL + xl}, zz

    inputs = [
        pltpu.make_async_copy(src, dst, in_sem.at[n])
        for n, (src, dst) in enumerate(((l_hbm, lv), (r_hbm, rv), (g_hbm, gv), (w_hbm, wv)))
    ]
    for c in inputs:
        c.start()

    barrier = pltpu.get_barrier_semaphore()

    def greet(device):
        pl.semaphore_signal(barrier, inc=1, device_id=device, device_id_type=MESH)

    def greet_all(at, first, last):
        def one(k, _):
            greet(at(k)[0])
            return 0

        lax.fori_loop(first, last, one, 0)

    greet(at_zx(FAR, 0))
    greet(at_zx(-FAR, 0))
    greet_all(row_at, 1, ROWS)
    for dz, dx in LAST + NEAR:
        greet(at_zx(-dz, dx))

    inputs[0].wait()
    inputs[1].wait()
    lf[...] = jnp.swapaxes(lv[...].astype(F32), 1, 2).reshape(256, 32)
    rf[...] = rv[...].reshape(256, 32).astype(F32)
    for i in range(32):
        lflat[:, 32 * i : 32 * i + 32] = lf[pl.ds(i, 8, stride=32), :]
    for j in range(16):
        rflat[:, 32 * j : 32 * j + 32] = rf[pl.ds(j, 16, stride=16), :]
    lb[col] = lflat[...].astype(BF)
    rb[row] = rflat[...].astype(BF)

    pl.semaphore_wait(barrier, GREETED)

    def left_copy(d, dz, dx):
        slot = ((z + ZS - d) % ZS) * XL + xl
        k = ((d + dz) % ZS) * XL + dx
        return pltpu.make_async_remote_copy(
            src_ref=lb.at[slot],
            dst_ref=lb.at[slot],
            send_sem=ag_l.at[0, k],
            recv_sem=ag_l.at[1, k],
            device_id=at_zx(dz, dx),
            device_id_type=MESH,
        )

    def left_arrived(k, wait):
        slot = ((z + ZS - k // XL) % ZS) * XL + (xl + k % XL) % XL
        c = pltpu.make_async_remote_copy(
            src_ref=lb.at[slot],
            dst_ref=lb.at[slot],
            send_sem=ag_l.at[0, k],
            recv_sem=ag_l.at[1, k],
            device_id=at_zx(0, 1),
            device_id_type=MESH,
        )
        wait(c)

    def spread(d):
        for dz, dx in NEAR:
            left_copy(d, dz, dx).start()

    def copies(at, n, src_slot, dst_slot, sems):
        def make(k):
            where, slot = at(k)
            return pltpu.make_async_remote_copy(
                src_ref=src_slot(slot),
                dst_ref=dst_slot,
                send_sem=sems.at[0, k],
                recv_sem=sems.at[1, k],
                device_id=where,
                device_id_type=MESH,
            )

        def each(act, first, last):
            def one(k, _):
                act(make(k))
                return 0

            lax.fori_loop(first, last, one, 0)

        return (
            lambda first=1, last=n: each(lambda c: c.start(), first, last),
            lambda first=1, last=n: each(lambda c: c.wait_recv(), first, last),
            lambda: each(lambda c: c.wait_send(), 1, n),
        )

    ag_r_start, ag_r_recv, ag_r_sent = copies(row_at, ROWS, lambda s: rb.at[row], rb.at[row], ag_r)
    rs_r_start, rs_r_recv, rs_r_sent = copies(row_at, ROWS, lambda s: sr.at[s], rr.at[row], rs_r)
    z_w_start, z_w_recv, z_w_sent = copies(z_at, ZS, lambda s: zb.at[z], zb.at[z], z_w)

    left_copy(0, FAR, 0).start()
    left_copy(0, -FAR, 0).start()
    ag_r_start()
    spread(0)

    inputs[2].wait()
    inputs[3].wait()
    gf[...] = gv[...].reshape(512, 128).astype(F32)
    for j in range(16):
        gji[32 * j : 32 * j + 32, :] = gf[pl.ds(j, 32, stride=16), :].astype(BF)
    gt[...] = gji[...].T
    expand(gji, wv, eb)

    left_arrived(FAR * XL, lambda c: c.wait_recv())
    for dz, dx in LAST:
        left_copy(FAR, dz, dx).start()
    spread(FAR)
    left_arrived((ZS - FAR) * XL, lambda c: c.wait_recv())
    spread(ZS - FAR)
    ag_r_recv()
    rg[...] = rb[...].reshape(256, 512)
    left_term(rg, eb, sl)

    zr, zq = z % 4, z // 4

    def group_copy(n):
        dz, dx = GROUP[n]
        return pltpu.make_async_remote_copy(
            src_ref=sl.at[(z + dz) % 4, (xl + dx) % XL],
            dst_ref=ra.at[n],
            send_sem=rs_a.at[0, n],
            recv_sem=rs_a.at[1, n],
            device_id=at_zx(dz, dx),
            device_id_type=MESH,
        )

    def rest(act):
        def one(k, _):
            left_arrived(k, act)
            return 0

        lax.fori_loop(1, FAR * XL, one, 0)
        lax.fori_loop(FAR * XL + 1, (ZS - FAR) * XL, one, 0)
        lax.fori_loop((ZS - FAR) * XL + 1, COLS, one, 0)

    rest(lambda c: c.wait_recv())
    for n in range(len(GROUP)):
        group_copy(n).start()
    lg[...] = lb[...].astype(F32).reshape(256, 1024).astype(BF)
    halves = pltpu.make_async_remote_copy(
        src_ref=wp, dst_ref=wq, send_sem=c_w.at[0], recv_sem=c_w.at[1], device_id=partner, device_id_type=MESH
    )
    wp[...] = outer_weight(1 - core, lg, rg, gt)
    halves.start()
    own_half = outer_weight(core, lg, rg, gt)
    halves.wait_recv()
    sw[...] = (own_half + wq[...]).astype(BF)

    def share_copy(k):
        where, slot = chip_at(k, 1)
        return pltpu.make_async_remote_copy(
            src_ref=sw.at[slot],
            dst_ref=rw.at[chip],
            send_sem=rs_w.at[0, k],
            recv_sem=rs_w.at[1, k],
            device_id=where,
            device_id_type=MESH,
        )

    def back_copy(k):
        return pltpu.make_async_remote_copy(
            src_ref=ab.at[core, chip],
            dst_ref=ab.at[core, chip],
            send_sem=ag_w.at[0, k],
            recv_sem=ag_w.at[1, k],
            device_id=chip_at(k, 1)[0],
            device_id_type=MESH,
        )

    def pass_on(k):
        slot = chip_at(k, -1)[1]
        return pltpu.make_async_remote_copy(
            src_ref=ab.at[core, slot],
            dst_ref=ab.at[core, slot],
            send_sem=f_w.at[0, k],
            recv_sem=f_w.at[1, k],
            device_id=partner,
            device_id_type=MESH,
        )

    for k in ACROSS:
        share_copy(k).start()
    rw[chip] = sw[chip]
    right_term(lg, eb, sr)
    rr[row] = sr[row]
    for k in ACROSS:
        share_copy(k).wait_recv()
    zb[z] = jnp.sum(rw[...].astype(F32), axis=0).astype(BF)
    z_w_start()
    rs_r_start()

    for n in range(len(GROUP)):
        group_copy(n).wait_recv()
    v = sl[zr, xl].astype(F32)
    for n in range(len(GROUP)):
        v = v + ra[n].astype(F32)
    sa[...] = v
    sb[...] = v.astype(BF)

    def far_copy(q):
        return pltpu.make_async_remote_copy(
            src_ref=sb.at[(zq + q) % 4],
            dst_ref=rl.at[q - 1],
            send_sem=rs_b.at[0, q],
            recv_sem=rs_b.at[1, q],
            device_id=at_zx(4 * q, 0),
            device_id_type=MESH,
        )

    z_w_recv(8, ZS)
    for q in (2, 1, 3):
        far_copy(q).start()

    z_w_recv(1, 8)
    ab[core, chip] = jnp.sum(zb[...].astype(F32), axis=0).astype(BF)
    for k in ACROSS:
        back_copy(k).start()
    pass_on(0).start()
    rs_r_recv()
    rflat[...] = jnp.sum(rr[...].astype(F32), axis=0)
    for j in range(16):
        ro[:, j, :] = rflat[:, 32 * j : 32 * j + 32]
    for k in ACROSS[::-1]:
        back_copy(k).wait_recv()
        pass_on(k).start()
    for q in (1, 2, 3):
        far_copy(q).wait_recv()
    lflat[...] = sa[zq] + rl[0].astype(F32) + rl[1].astype(F32) + rl[2].astype(F32)
    for i in range(32):
        lf[pl.ds(i, 8, stride=32), :] = lflat[:, 32 * i : 32 * i + 32]
    lo[...] = jnp.swapaxes(lf[...].reshape(8, 32, 32), 1, 2)
    for k in range(CHIPS):
        pass_on(k).wait_recv()
    wo[...] = ab[...].astype(F32).reshape(1024, 128) * (1.0 / 512)

    for done in (ag_r_sent, rs_r_sent, z_w_sent):
        done()
    halves.wait_send()
    for k in ACROSS:
        share_copy(k).wait_send()
        back_copy(k).wait_send()
    for k in range(CHIPS):
        pass_on(k).wait_send()
    rest(lambda c: c.wait_send())
    for d in (FAR, ZS - FAR):
        left_arrived(d * XL, lambda c: c.wait_send())
    for n in range(len(GROUP)):
        group_copy(n).wait_send()
    for q in (1, 2, 3):
        far_copy(q).wait_send()


def hand_over(l, r, w, lo, ro, wo, sem):
    moves = [pltpu.make_async_copy(a, b, sem.at[n]) for n, (a, b) in enumerate(((w, wo), (l, lo), (r, ro)))]
    for m in moves:
        m.start()
    for m in moves:
        m.wait()


def per_device(left_panel, right_panel, pair_grad, out_weight):
    V = pltpu.VMEM
    dma = pltpu.SemaphoreType.DMA
    args = [pltpu.with_memory_space_constraint(a, pltpu.HBM) for a in (left_panel, right_panel, pair_grad, out_weight)]
    raw = pl.pallas_call(
        kernel,
        out_shape=[
            jax.ShapeDtypeStruct((8, 32, 32), F32),
            jax.ShapeDtypeStruct((16, 16, 32), F32),
            jax.ShapeDtypeStruct((1024, 128), F32),
        ],
        in_specs=[pl.BlockSpec(memory_space=pltpu.HBM)] * 4,
        out_specs=[pl.BlockSpec(memory_space=V)] * 3,
        scratch_shapes=[
            V((8, 32, 32), BF), V((16, 16, 32), BF), V((32, 16, 128), BF), V((1024, 128), BF),
            V((256, 32), F32), V((256, 32), F32), V((512, 128), F32),
            V((8, 1024), F32), V((16, 512), F32), V((512, 128), BF), V((128, 512), BF),
            V((32, 8, 1024), BF), V((16, 16, 512), BF), V((256, 1024), BF), V((256, 512), BF), V((1024, 512), BF),
            V((4, 2, 4, 8, 1024), BF), V((7, 4, 8, 1024), BF), V((4, 8, 1024), F32), V((4, 8, 1024), BF), V((3, 8, 1024), BF),
            V((16, 16, 512), BF), V((16, 16, 512), BF),
            V((16, 32, 128), F32), V((16, 32, 128), F32), V((16, 32, 128), BF), V((16, 32, 128), BF), V((16, 32, 128), BF), V((2, 16, 32, 128), BF),
            dma((4,)), dma((2, 32)), dma((2, 16)), dma((2, 7)), dma((2, 4)), dma((2, 16)),
            dma((2,)), dma((2, 16)), dma((2, 16)), dma((2, 16)), dma((2, 16)),
        ],
        compiler_params=pltpu.CompilerParams(
            collective_id=0, has_side_effects=True, vmem_limit_bytes=24 << 20
        ),
        cost_estimate=pl.CostEstimate(flops=1 << 30, bytes_accessed=1 << 20, transcendentals=0),
        name="pair_backward",
    )(*args)
    shapes = [jax.ShapeDtypeStruct(a.shape, a.dtype) for a in raw]
    return pl.pallas_call(
        hand_over,
        out_shape=shapes,
        in_specs=[pl.BlockSpec(memory_space=V)] * 3,
        out_specs=[pl.BlockSpec(memory_space=pltpu.HBM)] * 3,
        scratch_shapes=[dma((3,))],
        name="hand_over",
    )(*[pltpu.with_memory_space_constraint(a, V) for a in raw])


def solution(mesh):
    in_specs = (P("col", "row", None), P("row", "col", None), P("row", "col", None), P())
    out_specs = (P("col", "row", None), P("row", "col", None), P())
    return jax.shard_map(
        per_device, mesh=mesh, in_specs=in_specs, out_specs=out_specs, check_vma=False
    )
```

```python
import jax
import jax.numpy as jnp
from jax import lax
from jax.experimental import pallas as pl
from jax.experimental.pallas import tpu as pltpu
from jax.sharding import PartitionSpec as P

MESH = pl.DeviceIdType.MESH
F32, BF = jnp.float32, jnp.bfloat16
ROWS, ZS, XL = 16, 16, 2
COLS = ZS * XL
CHIPS = 16
NEAR = ((2, 1), (-2, 1), (2, 0), (-2, 0), (1, 1), (-1, 1), (1, 0), (-1, 0), (0, 1))
FAR = 5
LAST = ((3, 1), (3, 0))
GREETED = len(NEAR) + 2 + len(LAST) + (ROWS - 1)
GROUP = ((2, 1), (2, 0), (1, 1), (-1, 1), (1, 0), (-1, 0), (0, 1))
ACROSS = (6, 5, 7, 10, 14, 2, 4, 9, 11, 13, 15, 1, 3, 8, 12)


def swap4(x):
    lane = lax.broadcasted_iota(jnp.int32, x[0].shape, 1)
    low = lane < 64
    even = (lane // 32) % 2 == 0
    r = [pltpu.roll(v, 64, 1) for v in x]
    a = [
        jnp.where(low, x[0], r[2]),
        jnp.where(low, x[1], r[3]),
        jnp.where(low, r[0], x[2]),
        jnp.where(low, r[1], x[3]),
    ]
    y = []
    for p in (0, 2):
        y.append(jnp.where(even, a[p], pltpu.roll(a[p + 1], 32, 1)))
        y.append(jnp.where(even, pltpu.roll(a[p], 96, 1), a[p + 1]))
    return y


def expand(gji, w, eb):
    wd = 256

    def part(a, _):
        w_rows = w[pl.ds(pl.multiple_of(a * wd, wd), wd), :]
        m = lax.dot_general(gji[...], w_rows, (((1,), (1,)), ((), ())), preferred_element_type=F32)
        m = (m * (1.0 / 256)).astype(BF)
        for h in range(wd // 128):
            for jg in range(4):
                for i0 in range(2):
                    x = []
                    for b in range(4):
                        r0 = (4 * jg + b) * 32 + 16 * i0
                        x.append(m[r0 : r0 + 16, 128 * h : 128 * h + 128])
                    y = swap4(x)
                    for q in range(4):
                        r0 = pl.multiple_of(a * wd + h * 128 + q * 32 + 16 * i0, 16)
                        eb[pl.ds(r0, 16), 128 * jg : 128 * jg + 128] = y[q]
        return 0

    lax.fori_loop(0, 1024 // wd, part, 0, unroll=4)


def left_term(rg, eb, out):
    wd = 256

    def part(t, _):
        rows = pl.ds(pl.multiple_of(t * wd, wd), wd)
        v = lax.dot_general(rg[...], eb[rows, :], (((1,), (1,)), ((), ())), preferred_element_type=F32)
        for m in range(4):
            out[:, :, m, :, rows] = v[64 * m : 64 * m + 64].reshape(4, 2, 8, wd).astype(BF)
        return 0

    lax.fori_loop(0, 1024 // wd, part, 0, unroll=4)


def right_term(lg, eb, out):
    wd = 256

    def part(t, _):
        cols = pl.ds(pl.multiple_of(t * wd, wd), wd)
        v = jnp.dot(lg[...], eb[:, cols], preferred_element_type=F32)
        out[:, :, cols] = v.reshape(16, 16, wd).astype(BF)
        return 0

    lax.fori_loop(0, 512 // wd, part, 0, unroll=2)


def outer_weight(half, lg, rg, gt):
    wd = 512
    o = lax.dot_general(
        lg[:, pl.ds(pl.multiple_of(half * wd, wd), wd)], rg[...], (((0,), (0,)), ((), ())), preferred_element_type=F32
    )
    o = (o * (1.0 / 256)).astype(BF)
    tiles = []
    for h in range(wd // 128):
        parts = [[None] * 2 for _ in range(16)]
        for jg in range(4):
            for i0 in range(2):
                x = []
                for q in range(4):
                    r0 = h * 128 + q * 32 + 16 * i0
                    x.append(o[r0 : r0 + 16, 128 * jg : 128 * jg + 128])
                y = swap4(x)
                for b in range(4):
                    parts[4 * jg + b][i0] = y[b]
        tiles.append(jnp.concatenate([p for q in parts for p in q], axis=0))
    v = jnp.dot(gt[...], jnp.concatenate(tiles, axis=1), preferred_element_type=F32).T
    return v.reshape(16, 32, 128)


def kernel(
    l_hbm, r_hbm, g_hbm, w_hbm, lo, ro, wo,
    lv, rv, gv, wv, lf, rf, gf, lflat, rflat, gji, gt,
    lb, rb, lg, rg, eb,
    sl, ra, sa, sb, rl, sr, rr, wp, wq, sw, rw, zb, ab,
    in_sem, ag_l, ag_r, rs_a, rs_b, rs_r, c_w, rs_w, z_w, ag_w, f_w,
):
    row, col = lax.axis_index("row"), lax.axis_index("col")
    z, xl = col // XL, col % XL
    xh, y, core = row // 8, (row // 2) % 4, row % 2
    chip = xl * 8 + row // 2
    partner = {"row": row + 1 - 2 * core, "col": col}

    def at_zx(dz, dx):
        c = ((z + dz) % ZS) * XL + (xl + dx) % XL
        return {"row": row, "col": c}

    def row_at(k):
        r = (row + k) % ROWS
        return {"row": r, "col": col}, r

    def chip_at(k, sign):
        r, x = ((xh + k // 4) % 2) * 4 + (y + sign * k) % 4, (xl + k // 8) % XL
        return {"row": r * 2 + core, "col": z * XL + x}, x * 8 + r

    def z_at(k):
        zz = (z + ZS // 2 + k // 2 * (1 - 2 * (1 - k % 2))) % ZS
        return {"row": row, "col": zz * XL + xl}, zz

    inputs = [
        pltpu.make_async_copy(src, dst, in_sem.at[n])
        for n, (src, dst) in enumerate(((l_hbm, lv), (r_hbm, rv), (g_hbm, gv), (w_hbm, wv)))
    ]
    for c in inputs:
        c.start()

    barrier = pltpu.get_barrier_semaphore()

    def greet(device):
        pl.semaphore_signal(barrier, inc=1, device_id=device, device_id_type=MESH)

    def greet_all(at, first, last):
        def one(k, _):
            greet(at(k)[0])
            return 0

        lax.fori_loop(first, last, one, 0)

    greet(at_zx(FAR, 0))
    greet(at_zx(-FAR, 0))
    greet_all(row_at, 1, ROWS)
    for dz, dx in LAST + NEAR:
        greet(at_zx(-dz, dx))

    inputs[0].wait()
    inputs[1].wait()
    lf[...] = jnp.swapaxes(lv[...].astype(F32), 1, 2).reshape(256, 32)
    rf[...] = rv[...].reshape(256, 32).astype(F32)
    for i in range(32):
        lflat[:, 32 * i : 32 * i + 32] = lf[pl.ds(i, 8, stride=32), :]
    for j in range(16):
        rflat[:, 32 * j : 32 * j + 32] = rf[pl.ds(j, 16, stride=16), :]
    lb[col] = lflat[...].astype(BF)
    rb[row] = rflat[...].astype(BF)

    pl.semaphore_wait(barrier, GREETED)

    def left_copy(d, dz, dx):
        slot = ((z + ZS - d) % ZS) * XL + xl
        k = ((d + dz) % ZS) * XL + dx
        return pltpu.make_async_remote_copy(
            src_ref=lb.at[slot],
            dst_ref=lb.at[slot],
            send_sem=ag_l.at[0, k],
            recv_sem=ag_l.at[1, k],
            device_id=at_zx(dz, dx),
            device_id_type=MESH,
        )

    def left_arrived(k, wait):
        slot = ((z + ZS - k // XL) % ZS) * XL + (xl + k % XL) % XL
        c = pltpu.make_async_remote_copy(
            src_ref=lb.at[slot],
            dst_ref=lb.at[slot],
            send_sem=ag_l.at[0, k],
            recv_sem=ag_l.at[1, k],
            device_id=at_zx(0, 1),
            device_id_type=MESH,
        )
        wait(c)

    def spread(d):
        for dz, dx in NEAR:
            left_copy(d, dz, dx).start()

    def copies(at, n, src_slot, dst_slot, sems):
        def make(k):
            where, slot = at(k)
            return pltpu.make_async_remote_copy(
                src_ref=src_slot(slot),
                dst_ref=dst_slot,
                send_sem=sems.at[0, k],
                recv_sem=sems.at[1, k],
                device_id=where,
                device_id_type=MESH,
            )

        def each(act, first, last):
            def one(k, _):
                act(make(k))
                return 0

            lax.fori_loop(first, last, one, 0)

        return (
            lambda first=1, last=n: each(lambda c: c.start(), first, last),
            lambda first=1, last=n: each(lambda c: c.wait_recv(), first, last),
            lambda: each(lambda c: c.wait_send(), 1, n),
        )

    ag_r_start, ag_r_recv, ag_r_sent = copies(row_at, ROWS, lambda s: rb.at[row], rb.at[row], ag_r)
    rs_r_start, rs_r_recv, rs_r_sent = copies(row_at, ROWS, lambda s: sr.at[s], rr.at[row], rs_r)
    z_w_start, z_w_recv, z_w_sent = copies(z_at, ZS, lambda s: zb.at[z], zb.at[z], z_w)

    left_copy(0, FAR, 0).start()
    left_copy(0, -FAR, 0).start()
    ag_r_start()
    spread(0)

    inputs[2].wait()
    inputs[3].wait()
    gf[...] = gv[...].reshape(512, 128).astype(F32)
    for j in range(16):
        gji[32 * j : 32 * j + 32, :] = gf[pl.ds(j, 32, stride=16), :].astype(BF)
    gt[...] = gji[...].T
    expand(gji, wv, eb)

    left_arrived(FAR * XL, lambda c: c.wait_recv())
    for dz, dx in LAST:
        left_copy(FAR, dz, dx).start()
    spread(FAR)
    left_arrived((ZS - FAR) * XL, lambda c: c.wait_recv())
    spread(ZS - FAR)
    ag_r_recv()
    rg[...] = rb[...].reshape(256, 512)
    left_term(rg, eb, sl)

    zr, zq = z % 4, z // 4

    def group_copy(n):
        dz, dx = GROUP[n]
        return pltpu.make_async_remote_copy(
            src_ref=sl.at[(z + dz) % 4, (xl + dx) % XL],
            dst_ref=ra.at[n],
            send_sem=rs_a.at[0, n],
            recv_sem=rs_a.at[1, n],
            device_id=at_zx(dz, dx),
            device_id_type=MESH,
        )

    def rest(act):
        def one(k, _):
            left_arrived(k, act)
            return 0

        lax.fori_loop(1, FAR * XL, one, 0)
        lax.fori_loop(FAR * XL + 1, (ZS - FAR) * XL, one, 0)
        lax.fori_loop((ZS - FAR) * XL + 1, COLS, one, 0)

    rest(lambda c: c.wait_recv())
    for n in range(len(GROUP)):
        group_copy(n).start()
    lg[...] = lb[...].astype(F32).reshape(256, 1024).astype(BF)
    halves = pltpu.make_async_remote_copy(
        src_ref=wp, dst_ref=wq, send_sem=c_w.at[0], recv_sem=c_w.at[1], device_id=partner, device_id_type=MESH
    )
    wp[...] = outer_weight(1 - core, lg, rg, gt)
    halves.start()
    own_half = outer_weight(core, lg, rg, gt)
    halves.wait_recv()
    sw[...] = (own_half + wq[...]).astype(BF)

    def share_copy(k):
        where, slot = chip_at(k, 1)
        return pltpu.make_async_remote_copy(
            src_ref=sw.at[slot],
            dst_ref=rw.at[chip],
            send_sem=rs_w.at[0, k],
            recv_sem=rs_w.at[1, k],
            device_id=where,
            device_id_type=MESH,
        )

    def back_copy(k):
        return pltpu.make_async_remote_copy(
            src_ref=ab.at[core, chip],
            dst_ref=ab.at[core, chip],
            send_sem=ag_w.at[0, k],
            recv_sem=ag_w.at[1, k],
            device_id=chip_at(k, 1)[0],
            device_id_type=MESH,
        )

    def pass_on(k):
        slot = chip_at(k, -1)[1]
        return pltpu.make_async_remote_copy(
            src_ref=ab.at[core, slot],
            dst_ref=ab.at[core, slot],
            send_sem=f_w.at[0, k],
            recv_sem=f_w.at[1, k],
            device_id=partner,
            device_id_type=MESH,
        )

    for k in ACROSS:
        share_copy(k).start()
    rw[chip] = sw[chip]
    right_term(lg, eb, sr)
    rr[row] = sr[row]
    for k in ACROSS:
        share_copy(k).wait_recv()
    zb[z] = jnp.sum(rw[...].astype(F32), axis=0).astype(BF)
    z_w_start()
    rs_r_start()

    for n in range(len(GROUP)):
        group_copy(n).wait_recv()
    v = sl[zr, xl].astype(F32)
    for n in range(len(GROUP)):
        v = v + ra[n].astype(F32)
    sa[...] = v
    sb[...] = v.astype(BF)

    def far_copy(q):
        return pltpu.make_async_remote_copy(
            src_ref=sb.at[(zq + q) % 4],
            dst_ref=rl.at[q - 1],
            send_sem=rs_b.at[0, q],
            recv_sem=rs_b.at[1, q],
            device_id=at_zx(4 * q, 0),
            device_id_type=MESH,
        )

    z_w_recv(8, ZS)
    for q in (2, 1, 3):
        far_copy(q).start()

    z_w_recv(1, 8)
    ab[core, chip] = jnp.sum(zb[...].astype(F32), axis=0).astype(BF)
    for k in ACROSS:
        back_copy(k).start()
    pass_on(0).start()
    rs_r_recv()
    rflat[...] = jnp.sum(rr[...].astype(F32), axis=0)
    for j in range(16):
        ro[:, j, :] = rflat[:, 32 * j : 32 * j + 32]
    for k in ACROSS[::-1]:
        back_copy(k).wait_recv()
        pass_on(k).start()

    def write_half(h):
        rows = pl.ds(pl.multiple_of(h * 512, 512), 512)
        wo[rows, :] = ab[h].astype(F32).reshape(512, 128) * (1.0 / 512)

    write_half(core)
    for q in (1, 2, 3):
        far_copy(q).wait_recv()
    lflat[...] = sa[zq] + rl[0].astype(F32) + rl[1].astype(F32) + rl[2].astype(F32)
    for i in range(32):
        lf[pl.ds(i, 8, stride=32), :] = lflat[:, 32 * i : 32 * i + 32]
    lo[...] = jnp.swapaxes(lf[...].reshape(8, 32, 32), 1, 2)
    for k in range(CHIPS):
        pass_on(k).wait_recv()
    write_half(1 - core)

    for done in (ag_r_sent, rs_r_sent, z_w_sent):
        done()
    halves.wait_send()
    for k in ACROSS:
        share_copy(k).wait_send()
        back_copy(k).wait_send()
    for k in range(CHIPS):
        pass_on(k).wait_send()
    rest(lambda c: c.wait_send())
    for d in (FAR, ZS - FAR):
        left_arrived(d * XL, lambda c: c.wait_send())
    for n in range(len(GROUP)):
        group_copy(n).wait_send()
    for q in (1, 2, 3):
        far_copy(q).wait_send()


def hand_over(l, r, w, lo, ro, wo, sem):
    moves = [pltpu.make_async_copy(a, b, sem.at[n]) for n, (a, b) in enumerate(((w, wo), (l, lo), (r, ro)))]
    for m in moves:
        m.start()
    for m in moves:
        m.wait()


def per_device(left_panel, right_panel, pair_grad, out_weight):
    V = pltpu.VMEM
    dma = pltpu.SemaphoreType.DMA
    args = [pltpu.with_memory_space_constraint(a, pltpu.HBM) for a in (left_panel, right_panel, pair_grad, out_weight)]
    raw = pl.pallas_call(
        kernel,
        out_shape=[
            jax.ShapeDtypeStruct((8, 32, 32), F32),
            jax.ShapeDtypeStruct((16, 16, 32), F32),
            jax.ShapeDtypeStruct((1024, 128), F32),
        ],
        in_specs=[pl.BlockSpec(memory_space=pltpu.HBM)] * 4,
        out_specs=[pl.BlockSpec(memory_space=V)] * 3,
        scratch_shapes=[
            V((8, 32, 32), BF), V((16, 16, 32), BF), V((32, 16, 128), BF), V((1024, 128), BF),
            V((256, 32), F32), V((256, 32), F32), V((512, 128), F32),
            V((8, 1024), F32), V((16, 512), F32), V((512, 128), BF), V((128, 512), BF),
            V((32, 8, 1024), BF), V((16, 16, 512), BF), V((256, 1024), BF), V((256, 512), BF), V((1024, 512), BF),
            V((4, 2, 4, 8, 1024), BF), V((7, 4, 8, 1024), BF), V((4, 8, 1024), F32), V((4, 8, 1024), BF), V((3, 8, 1024), BF),
            V((16, 16, 512), BF), V((16, 16, 512), BF),
            V((16, 32, 128), F32), V((16, 32, 128), F32), V((16, 32, 128), BF), V((16, 32, 128), BF), V((16, 32, 128), BF), V((2, 16, 32, 128), BF),
            dma((4,)), dma((2, 32)), dma((2, 16)), dma((2, 7)), dma((2, 4)), dma((2, 16)),
            dma((2,)), dma((2, 16)), dma((2, 16)), dma((2, 16)), dma((2, 16)),
        ],
        compiler_params=pltpu.CompilerParams(
            collective_id=0, has_side_effects=True, vmem_limit_bytes=24 << 20
        ),
        cost_estimate=pl.CostEstimate(flops=1 << 30, bytes_accessed=1 << 20, transcendentals=0),
        name="pair_backward",
    )(*args)
    shapes = [jax.ShapeDtypeStruct(a.shape, a.dtype) for a in raw]
    return pl.pallas_call(
        hand_over,
        out_shape=shapes,
        in_specs=[pl.BlockSpec(memory_space=V)] * 3,
        out_specs=[pl.BlockSpec(memory_space=pltpu.HBM)] * 3,
        scratch_shapes=[dma((3,))],
        name="hand_over",
    )(*[pltpu.with_memory_space_constraint(a, V) for a in raw])


def solution(mesh):
    in_specs = (P("col", "row", None), P("row", "col", None), P("row", "col", None), P())
    out_specs = (P("col", "row", None), P("row", "col", None), P())
    return jax.shard_map(
        per_device, mesh=mesh, in_specs=in_specs, out_specs=out_specs, check_vma=False
    )
```
